128 devices in a mesh: row: 16 (over x, y), col: 8 (over z, core).
Axes of the slice: x: 4, y: 4, z: 4, core: 2. Of those that a mesh axis runs over, the one named last changes fastest.
Arguments:
- excitation: float32 [2, 8, 131072], P(None, None, ('row', 'col')), may hold values from -6 to 6
- precond: float32 [131072], P(('row', 'col')), may hold values from 0.4 to 0.8
- near_blocks: bfloat16 [8, 1024, 2, 2, 128, 128], P('col', 'row')
- near_index: int32 [8, 1024, 2], P('col', 'row'), may hold values from 0 to 127, as said below
- coupling: bfloat16 [2048, 8, 2, 128, 128], P(('row', 'col')), may hold values from -0.1875 to 0.1875
- visible: int32 [2048, 8], P(('row', 'col')), may hold values from -1 to 1023, as said below
- reflect: float32 [2, 262144], P(None, ('row', 'col')), may hold values from -1 to 1
Outputs:
- currents: float32 [2, 8, 131072], P(None, None, ('row', 'col'))
- facet_currents: float32 [2, 8, 262144], P(None, None, ('row', 'col'))
The draws below stay inside these ranges and needn't reach their ends.
Inputs may be any that keep to these rules, and one draw needn't show every extreme that they name: `near_index`: within one column group every block row lists 2 different column blocks; on the column group that owns the block row's own unknowns, the first listed block is that diagonal block. `visible`: the tiles of one device never list a block twice, and list at most 2 blocks of any one device's 8 blocks (block b belongs to device b // 8 along row+col); some device's tiles list exactly 2 blocks of some device. The tiles of one device see the blocks of at most 64 devices.
All inputs are finite; a program needn't handle non-finite values.
Results may differ from the reference program's by a relative error of at most 0.0048.
Values may be sent and summed in bfloat16 or wider, within the bound.
No kernel may reach another device: no remote copies, remote signals or barrier semaphores. Data moves between devices by JAX's collectives and lax.ppermute only.
A program may use at most 128 MiB of HBM per device.

```python
import math
import jax
import jax.numpy as jnp
from jax import lax

N = 131072
BS = 128
EXC = 8
KB = 2
FT = 128
VB = 8
TILES_DEV = 16
CAP = 2
ITERS = 2
NB = 1024
SEGB = 8
TILES = 2048
FACETS = 262144
SRC_MAX = 64
N_COL = 8
DEVICES = 128


def draw_near_blocks(key, part):
    key = jax.random.fold_in(key, 7)
    key_vals, key_real, key_imag = jax.random.split(key, 3)
    shape = (N_COL, NB, KB, 2, BS, BS)
    scale = 0.5 / math.sqrt(BS * KB * N_COL)
    values = jax.random.normal(key_vals, shape, jnp.float32) * scale
    diag_real = jax.random.uniform(key_real, (N_COL, NB, 1, 1, BS, 1), jnp.float32, 1.0, 2.0)
    diag_imag = jax.random.uniform(key_imag, (N_COL, NB, 1, 1, BS, 1), jnp.float32, -0.5, 0.5)
    diag_vals = jnp.concatenate([diag_real, diag_imag], axis=3)
    block_rows = jnp.arange(NB, dtype=jnp.int32)
    owner = block_rows // SEGB % N_COL
    owned = (jnp.arange(N_COL, dtype=jnp.int32)[:, None] == owner[None, :])[:, :, None, None, None, None]
    first = (jnp.arange(KB, dtype=jnp.int32) == 0)[None, None, :, None, None, None]
    ident = (jnp.arange(BS)[:, None] == jnp.arange(BS)[None, :])[None, None, None, None, :, :]
    values = jnp.where(owned & first & ident, values + diag_vals, values)
    return values.astype(jnp.bfloat16)


def draw_near_index(key, part):
    key = jax.random.fold_in(key, 11)
    group_blocks = NB // N_COL
    scores = jax.random.randint(key, (N_COL, NB, group_blocks - 1), 0, 2 ** 16, jnp.int32) * (group_blocks - 1) + jnp.arange(group_blocks - 1, dtype=jnp.int32)
    order = jnp.argsort(scores, axis=2)[:, :, :KB].astype(jnp.int32)
    block_rows = jnp.arange(NB, dtype=jnp.int32)
    segment = block_rows // SEGB
    self_local = segment // N_COL * SEGB + block_rows % SEGB
    owner = segment % N_COL
    entries = (self_local[None, :, None] + 1 + order) % group_blocks
    owned = jnp.arange(N_COL, dtype=jnp.int32)[:, None] == owner[None, :]
    leading = jnp.where(owned, self_local[None, :], entries[:, :, 0])
    entries = entries.at[:, :, 0].set(leading)
    return entries.astype(jnp.int32)


def draw_visible(key, part):
    key = jax.random.fold_in(key, 23)
    key_rank, key_src, key_slot, key_shuffle = jax.random.split(key, 4)
    count = TILES_DEV * VB
    lowest = SRC_MAX // 2
    dev_rank = jnp.argsort(jax.random.randint(key_rank, (DEVICES,), 0, 2 ** 20, jnp.int32) * DEVICES + jnp.arange(DEVICES, dtype=jnp.int32)).astype(jnp.int32)
    live_sources = lowest + (SRC_MAX - lowest) * dev_rank // max(DEVICES - 1, 1)
    src_order = jnp.argsort(jax.random.randint(key_src, (DEVICES, DEVICES), 0, 2 ** 16, jnp.int32) * DEVICES + jnp.arange(DEVICES, dtype=jnp.int32), axis=1).astype(jnp.int32)
    slot_order = jnp.argsort(jax.random.randint(key_slot, (DEVICES, DEVICES, SEGB), 0, 2 ** 16, jnp.int32) * SEGB + jnp.arange(SEGB, dtype=jnp.int32), axis=2).astype(jnp.int32)
    position = jnp.arange(count, dtype=jnp.int32)
    which = jnp.minimum(position // CAP, DEVICES - 1)
    turn = position % CAP
    source = src_order[:, which]
    slot_pick = slot_order[jnp.arange(DEVICES)[:, None], source, turn[None, :]]
    block_ids = jnp.where((position // CAP)[None, :] < live_sources[:, None], source * SEGB + slot_pick, -1)
    shuffle = jnp.argsort(jax.random.randint(key_shuffle, (DEVICES, count), 0, 2 ** 16, jnp.int32) * count + position, axis=1)
    block_ids = jnp.take_along_axis(block_ids, shuffle, axis=1)
    return block_ids.reshape(TILES, VB).astype(jnp.int32)


def block_scale(rng, dims, cuts, low, largest):
    def one(dim, blocks):
        heights = jax.random.uniform(jax.random.fold_in(jax.random.fold_in(rng, 6), dim), (blocks,), jnp.float32, low / len(cuts), largest / len(cuts))
        return jnp.repeat(jnp.exp(heights), dims[dim] // blocks).reshape((-1,) + (1,) * (len(dims) - dim - 1))

    gain = one(*cuts[0])
    for cut in cuts[1:]:
        gain = gain * one(*cut)
    return gain


def centred(rng, shape, width, reach, cuts=(), held_as=jnp.bfloat16):
    drawn = width * jax.random.normal(rng, shape, jnp.float32)
    if cuts:
        drawn = drawn * block_scale(rng, shape, cuts, -0.22, 0.18)
    return jnp.clip(drawn, -reach, reach).astype(held_as)


def setup_inputs(seed: int = 0) -> dict:
    arg_keys = jax.random.split(jax.random.key(seed), 8)
    return {
        "excitation": centred(arg_keys[0], (2, EXC, N), 1.0, 6.0, ((2, 128),), jnp.float32),
        "precond": jnp.clip(jnp.exp(math.log(0.8) - 0.6931472 * jax.random.uniform(arg_keys[1], (N,), jnp.float32) ** block_scale(arg_keys[1], (N,), ((0, 128),), -0.2, 0.2)), 0.4, 0.8),
        "near_blocks": draw_near_blocks(jax.random.fold_in(arg_keys[7], 71), 0),
        "near_index": draw_near_index(jax.random.fold_in(arg_keys[7], 71), 0),
        "coupling": centred(arg_keys[4], (TILES, VB, 2, FT, BS), (FT * VB) ** -0.5, 0.1875, ((0, 128),)),
        "visible": draw_visible(jax.random.fold_in(arg_keys[7], 71), 0),
        "reflect": jnp.clip(jax.random.uniform(arg_keys[6], (2, FACETS), jnp.float32, -1.0, 1.0) * block_scale(arg_keys[6], (2, FACETS), ((1, 128),), -0.4, 0.0), -1.0, 1.0),
    }


def reference(excitation, precond, near_blocks, near_index, coupling, visible, reflect):
    col_ids = jnp.arange(N_COL, dtype=jnp.int32)
    global_cols = ((near_index // SEGB) * N_COL + col_ids[:, None, None]) * SEGB + near_index % SEGB
    coupling_dev = coupling.reshape(DEVICES, TILES_DEV, VB, 2, FT, BS)
    visible_dev = visible.reshape(DEVICES, TILES_DEV, VB)
    reflect_dev = jnp.transpose(reflect.reshape(2, DEVICES, TILES_DEV, FT), (1, 0, 2, 3))

    def near_field(blocks):
        def one_col(args):
            zblock, gcols = args
            chosen = blocks[:, :, gcols, :].astype(jnp.float32)
            prod = jnp.einsum("bkpij,qebkj->pqebi", zblock.astype(jnp.float32), chosen)
            return jnp.stack([prod[0, 0] - prod[1, 1], prod[0, 1] + prod[1, 0]])
        terms = lax.map(one_col, (near_blocks, global_cols))
        return jnp.sum(terms, axis=0).reshape(2, EXC, N)

    def optics(blocks):
        def one_dev(carry, args):
            couple, seen, coeff = args
            is_live = seen >= 0
            safe_ids = jnp.where(is_live, seen, 0)
            entries = blocks[:, :, safe_ids, :].astype(jnp.float32)
            entries = jnp.where(is_live[None, None, :, :, None], entries, 0.0)
            couple32 = couple.astype(jnp.float32)
            inc = jnp.einsum("tvpfj,qetvj->pqtef", couple32, entries)
            inc_re = inc[0, 0] - inc[1, 1]
            inc_im = inc[0, 1] + inc[1, 0]
            coef_re = coeff[0][:, None, :]
            coef_im = coeff[1][:, None, :]
            facets = jnp.stack([coef_re * inc_re - coef_im * inc_im, coef_re * inc_im + coef_im * inc_re])
            facet_rounded = lax.optimization_barrier(facets.astype(jnp.bfloat16)).astype(jnp.float32)
            back = jnp.einsum("tvpfj,qtef->pqtvej", couple32, facet_rounded)
            back = jnp.stack([back[0, 0] - back[1, 1], back[0, 1] + back[1, 0]])
            back = jnp.where(is_live[None, :, :, None, None], back, 0.0)
            values = jnp.transpose(back.reshape(2, TILES_DEV * VB, EXC, BS), (0, 2, 1, 3))
            carry = carry.at[:, :, safe_ids.reshape(-1), :].add(values)
            return carry, facets
        start = jnp.zeros((2, EXC, NB, BS), jnp.float32)
        back, facets = lax.scan(one_dev, start, (coupling_dev, visible_dev, reflect_dev))
        facets = jnp.transpose(facets, (1, 3, 0, 2, 4)).reshape(2, EXC, FACETS)
        return back.reshape(2, EXC, N), facets

    currents = precond[None, None, :] * excitation
    facet_out = jnp.zeros((2, EXC, FACETS), jnp.float32)
    for iteration in range(ITERS):
        rounded = lax.optimization_barrier(currents.astype(jnp.bfloat16))
        blocks = rounded.reshape(2, EXC, NB, BS)
        near = near_field(blocks)
        back, facet_out = optics(blocks)
        currents = currents + precond[None, None, :] * (excitation - near - back)
    return currents, facet_out
```

```python
import functools

import jax
import jax.numpy as jnp
from jax import lax
from jax.experimental import pallas as pl
from jax.experimental.pallas import tpu as pltpu
from jax.sharding import PartitionSpec as P

ITERS = 2
TURNS = 2
VMEM = pl.BlockSpec(memory_space=pltpu.VMEM)
SMEM = pl.BlockSpec(memory_space=pltpu.SMEM)


def params(mib, **more):
    return pltpu.CompilerParams(vmem_limit_bytes=mib << 20, **more)


def dot_t(a, b):
    return lax.dot_general(a, b, (((1,), (1,)), ((), ())), preferred_element_type=jnp.float32)


def slots_kernel(rows, cols, seg, me_ref, visible_ref, forward_ref, back_ref, wanted_ref, count_ref):
    tiles, slots = visible_ref.shape
    me = me_ref[0]
    none = rows * cols

    def clear(i, _):
        count_ref[i] = 0
        return 0

    lax.fori_loop(0, none + 1, clear, 0, unroll=8)

    def clear_wanted(i, _):
        for j in range(rows * TURNS):
            wanted_ref[i, j] = seg
        return 0

    lax.fori_loop(0, cols, clear_wanted, 0)

    def tile(t, _):
        for v in range(slots):
            block = visible_ref[t, v]
            entry = t * slots + v
            live = block >= 0
            owner = jnp.where(live, lax.shift_right_arithmetic(block, log2(seg)), none)
            turn = count_ref[owner]
            count_ref[owner] = turn + live.astype(jnp.int32)
            row = lax.shift_right_arithmetic(owner, log2(cols))
            col = owner & (cols - 1)
            place = row * TURNS + turn
            forward_ref[entry] = jnp.where(live, col * (rows * TURNS) + place, -1)
            back_ref[entry] = jnp.where(live, owner * TURNS + turn, -1)
            line = jnp.where(live, (col - me) & (cols - 1), cols)
            wanted_ref[line, jnp.where(live, place, 0)] = block & (seg - 1)
        return 0

    lax.fori_loop(0, tiles, tile, 0)

    def find(i, free):
        return jnp.where(count_ref[i] < TURNS, i * TURNS + TURNS - 1, free)

    back_ref[tiles * slots] = lax.fori_loop(0, none, find, 0, unroll=8)


def log2(n):
    return n.bit_length() - 1


def make_slots(me, visible, rows, cols, seg):
    count = visible.size
    return pl.pallas_call(
        functools.partial(slots_kernel, rows, cols, seg),
        out_shape=(
            jax.ShapeDtypeStruct((count,), jnp.int32),
            jax.ShapeDtypeStruct((count + 1,), jnp.int32),
            jax.ShapeDtypeStruct((cols + 1, 128), jnp.int32),
        ),
        in_specs=[SMEM, SMEM],
        out_specs=(SMEM, SMEM, SMEM),
        scratch_shapes=[pltpu.SMEM((rows * cols + 1,), jnp.int32)],
        name="slots",
    )(me, visible)


def send_kernel(me_ref, index_ref, wanted_ref, blocks_ref, group_ref, *rest):
    count, per_row, _, size, _ = blocks_ref.shape
    tag_ref = rest[0] if len(rest) == 3 else None
    out_ref, own_ref = rest[-2:]
    exc = own_ref.shape[1]
    half = exc // 2
    me = me_ref[0]
    peers = pl.num_programs(0)
    p = pl.program_id(0)
    line = ((me - p) & (peers - 1)) * 128
    slots = group_ref.shape[0] * TURNS
    for s in range(slots):
        block = wanted_ref[line + s] & (count - 1)
        out_ref[0, s] = group_ref[s // TURNS, pl.ds(pl.multiple_of(block * exc, exc), exc), :]
    if tag_ref is not None:
        out_ref[0, slots + count] = tag_ref[0]
    for i in range(count):
        parts = []
        for k in range(per_row):
            block = index_ref[(p * count + i) * per_row + k]
            place = pl.multiple_of((block & (count - 1)) * exc, exc)
            parts.append(
                group_ref[lax.shift_right_arithmetic(block, log2(count)), pl.ds(place, exc), :]
            )
        weights = [blocks_ref[i, k].reshape(2 * size, size) for k in range(per_row)]
        total = dot_t(jnp.concatenate(parts, axis=1), jnp.concatenate(weights, axis=1))
        by_re, by_im = total[:, :size], total[:, size:]
        sums = jnp.concatenate([by_re[:half] - by_im[half:], by_re[half:] + by_im[:half]], axis=0)
        out_ref[0, slots + i] = jnp.where(p == me, 0.0, sums).astype(jnp.bfloat16)
        own_ref[i] = jnp.where(p == me, sums, own_ref[i])


def send(me, index, wanted, blocks, group, tags, seg, exc):
    rows, per_row, _, size, _ = blocks.shape
    cols = rows // seg
    slots = group.shape[0] * TURNS + seg + (tags is not None)
    in_specs = [
        pl.BlockSpec((seg, per_row, 2, size, size), lambda i, *s: (i, 0, 0, 0, 0)),
        pl.BlockSpec(group.shape, lambda i, *s: (0, 0, 0)),
    ]
    operands = [blocks, group]
    if tags is not None:
        in_specs.append(pl.BlockSpec((1, exc, size), lambda i, *s: (i, 0, 0)))
        operands.append(tags)
    return pl.pallas_call(
        send_kernel,
        out_shape=(
            jax.ShapeDtypeStruct((cols, slots, exc, size), jnp.bfloat16),
            jax.ShapeDtypeStruct((seg, exc, size), jnp.float32),
        ),
        grid_spec=pltpu.PrefetchScalarGridSpec(
            num_scalar_prefetch=3,
            grid=(cols,),
            in_specs=in_specs,
            out_specs=(
                pl.BlockSpec((1, slots, exc, size), lambda i, *s: (i, 0, 0, 0)),
                pl.BlockSpec((seg, exc, size), lambda i, *s: (0, 0, 0)),
            ),
        ),
        compiler_params=params(57),
        cost_estimate=pl.CostEstimate(
            flops=2 * exc * blocks.size, bytes_accessed=2 * blocks.size, transcendentals=0
        ),
        name="send",
    )(me, index, wanted, *operands)


def optics_kernel(forward_ref, back_ref, coupling_ref, x_ref, own_ref, reflect_ref, facet_ref, out_ref, near_ref):
    tiles, slots, _, facets, size = coupling_ref.shape
    cols = x_ref.shape[0]
    seg, exc = own_ref.shape[:2]
    half = exc // 2
    step = pl.program_id(0)
    places = out_ref.shape[0] // cols
    free = back_ref[back_ref.shape[0] - 1]

    @pl.when(step == 0)
    def _():
        for b in range(seg):
            total = own_ref[b]
            for c in range(cols):
                total += x_ref[c, places + b].astype(jnp.float32)
            near_ref[b] = total

    for t in range(tiles):
        first = (step * tiles + t) * slots
        total = None
        weights = []
        for v in range(0, slots, 2):
            parts = []
            for u in (v, v + 1):
                slot = forward_ref[first + u]
                live = slot >= 0
                slot = jnp.where(live, slot, 0)
                x = x_ref[lax.shift_right_arithmetic(slot, log2(places)), slot & (places - 1)]
                parts.append(jnp.where(live, x, jnp.zeros_like(x)))
            weights.append(
                jnp.concatenate(
                    [coupling_ref[t, u].reshape(2 * facets, size) for u in (v, v + 1)], axis=1
                )
            )
            product = dot_t(jnp.concatenate(parts, axis=1), weights[-1])
            total = product if total is None else total + product
        by_re, by_im = total[:, :facets], total[:, facets:]
        inc_re = by_re[:half] - by_im[half:]
        inc_im = by_re[half:] + by_im[:half]
        lanes = slice(t * facets, (t + 1) * facets)
        coef_re, coef_im = reflect_ref[0:1, lanes], reflect_ref[1:2, lanes]
        out_re = coef_re * inc_re - coef_im * inc_im
        out_im = coef_re * inc_im + coef_im * inc_re
        facet_ref[0, :, lanes] = out_re
        facet_ref[1, :, lanes] = out_im
        both = jnp.concatenate(
            [
                jnp.concatenate([out_re, -out_im], axis=1),
                jnp.concatenate([out_im, out_re], axis=1),
            ],
            axis=0,
        ).astype(jnp.bfloat16)
        for v in range(0, slots, 2):
            sums = jnp.dot(both, weights[v // 2], preferred_element_type=jnp.float32)
            sums = sums.astype(jnp.bfloat16)
            for u in range(2):
                slot = back_ref[first + v + u]
                out_ref[jnp.where(slot >= 0, slot, free)] = sums[:, u * size : (u + 1) * size]


def optics(forward, back, coupling, x, own, reflect, devices):
    tiles, slots, _, facets, size = coupling.shape
    exc = x.shape[2]
    step = 2
    return pl.pallas_call(
        optics_kernel,
        out_shape=(
            jax.ShapeDtypeStruct((2, exc // 2, tiles * facets), jnp.float32),
            jax.ShapeDtypeStruct((devices * TURNS, exc, size), jnp.bfloat16),
            jax.ShapeDtypeStruct(own.shape, jnp.float32),
        ),
        grid_spec=pltpu.PrefetchScalarGridSpec(
            num_scalar_prefetch=2,
            grid=(tiles // step,),
            in_specs=[
                pl.BlockSpec((step, slots, 2, facets, size), lambda i, *s: (i, 0, 0, 0, 0)),
                pl.BlockSpec(x.shape, lambda i, *s: (0, 0, 0, 0)),
                pl.BlockSpec(own.shape, lambda i, *s: (0, 0, 0)),
                pl.BlockSpec((2, step * facets), lambda i, *s: (0, i)),
            ],
            out_specs=(
                pl.BlockSpec((2, exc // 2, step * facets), lambda i, *s: (0, 0, i)),
                pl.BlockSpec((devices * TURNS, exc, size), lambda i, *s: (0, 0, 0)),
                pl.BlockSpec(own.shape, lambda i, *s: (0, 0, 0)),
            ),
        ),
        compiler_params=params(57),
        cost_estimate=pl.CostEstimate(
            flops=4 * exc * coupling.size, bytes_accessed=2 * coupling.size, transcendentals=0
        ),
        name="optics",
    )(forward, back, coupling, x, own, reflect)


def update_kernel(cols, owner_ref, back_ref, near_ref, currents_ref, excitation_ref, precond_ref, out_ref, *rest):
    count, exc, size = back_ref.shape
    seg = near_ref.shape[0]
    half = exc // 2
    total_ref = rest[-1]
    total_ref[:seg] = near_ref[...]
    rows = count // (cols * TURNS)

    def add(r, _):
        for c in range(cols):
            for turn in range(TURNS):
                block = owner_ref[(c * rows + r) * TURNS + turn]
                slot = (r * cols + c) * TURNS + turn
                total_ref[block] = total_ref[block] + back_ref[slot].astype(jnp.float32)
        return 0

    lax.fori_loop(0, rows, add, 0)
    for b in range(seg):
        lanes = slice(b * size, (b + 1) * size)
        scale = precond_ref[:, lanes]
        for q in range(2):
            part = total_ref[b, q * half : (q + 1) * half]
            new = currents_ref[q, :, lanes] + scale * (excitation_ref[q, :, lanes] - part)
            out_ref[q, :, lanes] = new
            if len(rest) > 1:
                total_ref[b, q * half : (q + 1) * half] = new
    if len(rest) > 1:
        copies_ref = rest[0]
        rounded = total_ref[:seg].astype(jnp.bfloat16).reshape(seg * exc, size)
        for r in range(copies_ref.shape[0]):
            copies_ref[r] = rounded


def update(owner, back, near, currents, excitation, precond, copies, cols):
    seg, exc, size = near.shape
    out_shape = [jax.ShapeDtypeStruct(currents.shape, jnp.float32)]
    if copies:
        out_shape.append(jax.ShapeDtypeStruct((copies, seg * exc, size), jnp.bfloat16))
    return pl.pallas_call(
        functools.partial(update_kernel, cols),
        out_shape=out_shape,
        in_specs=[SMEM] + [VMEM] * 5,
        out_specs=[VMEM] * len(out_shape),
        scratch_shapes=[pltpu.VMEM((seg + 1, exc, size), jnp.float32)],
        compiler_params=params(16),
        name="update",
    )(owner, back, near, currents, excitation, precond[None, :])


def shards(excitation, precond, near_blocks, near_index, coupling, visible, reflect):
    exc = 2 * excitation.shape[1]
    size = coupling.shape[-1]
    seg = excitation.shape[2] // size
    rows, cols = lax.axis_size("row"), lax.axis_size("col")
    devices = rows * cols

    me = lax.axis_index("col").astype(jnp.int32).reshape(1)
    forward, back, wanted = make_slots(me, visible, rows, cols, seg)
    mine = lax.dynamic_slice_in_dim(
        jnp.concatenate([wanted[:cols], wanted[:cols]]), cols - me[0], cols, axis=0
    )
    tags = jnp.transpose(mine[:, : rows * TURNS].reshape(cols, rows, TURNS), (1, 0, 2))
    tags = jnp.repeat(tags.astype(jnp.bfloat16), size // TURNS, axis=2)
    tags = jnp.concatenate([tags, jnp.zeros((rows, exc - cols, size), jnp.bfloat16)], axis=1)

    currents = precond[None, None, :] * excitation
    rounded = currents.astype(jnp.bfloat16).reshape(2, exc // 2, seg, size)
    rounded = jnp.transpose(rounded, (2, 0, 1, 3)).reshape(1, seg * exc, size)
    copies = jnp.concatenate(
        [jnp.broadcast_to(rounded, (rows,) + rounded.shape[1:]), tags], axis=1
    )
    lines = [wanted[:1]]
    for k in range(1, cols):
        with jax.named_scope("wanted_exchange"):
            ring = [(i, (i + k) % cols) for i in range(cols)]
            lines.append(lax.ppermute(wanted[k : k + 1], "col", ring))
    wanted = jnp.concatenate(lines).reshape(-1)
    index = near_index[0].reshape(-1)
    owner = None
    for iteration in range(ITERS):
        last = iteration == ITERS - 1
        with jax.named_scope("row_exchange"):
            group = lax.all_to_all(copies, "row", 0, 0, tiled=True)
        tags = None
        if iteration == 0:
            tags = jnp.transpose(group[:, seg * exc : seg * exc + cols], (1, 0, 2))
        packed, own = send(me, index, wanted, near_blocks[0], group, tags, seg, exc)
        with jax.named_scope("col_exchange"):
            x = lax.all_to_all(packed, "col", 0, 0, tiled=True)
        if iteration == 0:
            owner = x[:, -1, :, :: size // TURNS].astype(jnp.int32).reshape(-1)
        facets, sums, near = optics(forward, back, coupling, x, own, reflect, devices)
        with jax.named_scope("back_exchange"):
            sums = lax.all_to_all(
                sums.reshape(devices, TURNS * exc, size), ("row", "col"), 0, 0, tiled=True
            )
        sums = sums.reshape(devices * TURNS, exc, size)
        out = update(
            owner, sums, near, currents, excitation, precond, 0 if last else rows, cols
        )
        currents = out[0]
        copies = None if last else out[1]
    return currents, facets


def solution(mesh):
    placed = (
        P(None, None, ("row", "col")),
        P(("row", "col")),
        P("col", "row", None, None, None, None),
        P("col", "row", None),
        P(("row", "col"), None, None, None, None),
        P(("row", "col"), None),
        P(None, ("row", "col")),
    )
    return jax.shard_map(
        shards,
        mesh=mesh,
        in_specs=placed,
        out_specs=(P(None, None, ("row", "col")), P(None, None, ("row", "col"))),
        check_vma=False,
    )
```

```python
import functools

import jax
import jax.numpy as jnp
from jax import lax
from jax.experimental import pallas as pl
from jax.experimental.pallas import tpu as pltpu
from jax.sharding import PartitionSpec as P

ITERS = 2
TURNS = 2
VMEM = pl.BlockSpec(memory_space=pltpu.VMEM)
SMEM = pl.BlockSpec(memory_space=pltpu.SMEM)
HBM = pl.BlockSpec(memory_space=pltpu.HBM)


def params(mib, **more):
    return pltpu.CompilerParams(vmem_limit_bytes=mib << 20, **more)


def dot_t(a, b):
    return lax.dot_general(a, b, (((1,), (1,)), ((), ())), preferred_element_type=jnp.float32)


def log2(n):
    return n.bit_length() - 1


def start_kernel(
    rows, cols, me_ref, visible_in, excitation_in, precond_in,
    forward_out, back_out, wanted_ref, currents_ref, copies_ref,
    count_ref, code_ref, visible_ref, excitation_ref, precond_ref, forward_ref, back_ref, sems,
):
    fetches = [
        pltpu.make_async_copy(visible_in, visible_ref, sems.at[0]),
        pltpu.make_async_copy(excitation_in, excitation_ref, sems.at[1]),
        pltpu.make_async_copy(precond_in, precond_ref, sems.at[2]),
    ]
    stores = [
        pltpu.make_async_copy(forward_ref, forward_out, sems.at[3]),
        pltpu.make_async_copy(back_ref, back_out, sems.at[4]),
    ]
    for fetch in fetches:
        fetch.start()
    slots, tiles = visible_ref.shape
    half, lanes = excitation_ref.shape[1:]
    size = copies_ref.shape[2]
    seg, exc = lanes // size, 2 * half
    me = me_ref[0]
    none = rows * cols
    base = 2 * seg

    def clear(i, _):
        count_ref[i] = 0
        code_ref[i] = seg * base + seg
        return 0

    lax.fori_loop(0, none + 1, clear, 0, unroll=8)
    fetches[0].wait()

    def tile(t, _):
        for v in range(slots):
            block = visible_ref[v, t]
            entry = t * slots + v
            live = block >= 0
            owner = jnp.where(live, lax.shift_right_arithmetic(block, log2(seg)), none)
            turn = count_ref[owner]
            count_ref[owner] = turn + live.astype(jnp.int32)
            row = lax.shift_right_arithmetic(owner, log2(cols))
            col = owner & (cols - 1)
            place = row * TURNS + turn
            forward_ref[entry] = jnp.where(live, col * (rows * TURNS + 1) + place, -1)
            back_ref[entry] = jnp.where(live, owner * TURNS + turn, -1)
            line = jnp.where(live, (col - me) & (cols - 1), cols)
            mine = block & (seg - 1)
            wanted_ref[line, jnp.where(live, place, 0)] = mine
            code_ref[owner] = code_ref[owner] + jnp.where(turn == 0, base, 1) * (mine - seg)
        return 0

    lax.fori_loop(0, tiles, tile, 0)

    def find(i, free):
        return jnp.where(count_ref[i] < TURNS, i * TURNS + TURNS - 1, free)

    back_ref[tiles * slots] = lax.fori_loop(0, none, find, 0, unroll=8)
    for store in stores:
        store.start()
    for fetch in fetches[1:]:
        fetch.wait()
    parts = []
    for b in range(seg):
        at = slice(b * size, (b + 1) * size)
        for q in range(2):
            new = precond_ref[:, at] * excitation_ref[q, :, at]
            currents_ref[q, :, at] = new
            parts.append(new)
    rounded = jnp.concatenate(parts, axis=0).astype(jnp.bfloat16)
    line = lax.broadcasted_iota(jnp.int32, (exc, size), 0)

    def fill(r, _):
        tag = jnp.zeros((exc, size), jnp.float32)
        for c in range(cols):
            tag = jnp.where(line == c, code_ref[r * cols + c].astype(jnp.float32), tag)
        copies_ref[r, : seg * exc] = rounded
        copies_ref[r, seg * exc :] = tag.astype(jnp.bfloat16)
        return 0

    lax.fori_loop(0, rows, fill, 0)
    for store in stores:
        store.wait()


def start(me, visible, excitation, precond, rows, cols, size):
    count = visible.size
    exc = 2 * excitation.shape[1]
    lines = excitation.shape[2] // size * exc
    return pl.pallas_call(
        functools.partial(start_kernel, rows, cols),
        out_shape=(
            jax.ShapeDtypeStruct((count,), jnp.int32),
            jax.ShapeDtypeStruct((count + 1,), jnp.int32),
            jax.ShapeDtypeStruct((cols + 1, 128), jnp.int32),
            jax.ShapeDtypeStruct(excitation.shape, jnp.float32),
            jax.ShapeDtypeStruct((rows, lines + exc, size), jnp.bfloat16),
        ),
        in_specs=[SMEM, HBM, HBM, HBM],
        out_specs=(HBM, HBM, SMEM, VMEM, VMEM),
        compiler_params=params(64),
        scratch_shapes=[
            pltpu.SMEM((rows * cols + 1,), jnp.int32),
            pltpu.SMEM((rows * cols + 1,), jnp.int32),
            pltpu.SMEM(visible.shape[::-1], jnp.int32),
            pltpu.VMEM(excitation.shape, jnp.float32),
            pltpu.VMEM((1, precond.size), jnp.float32),
            pltpu.SMEM((count,), jnp.int32),
            pltpu.SMEM((count + 1,), jnp.int32),
            pltpu.SemaphoreType.DMA((5,)),
        ],
        name="start",
    )(me, visible.T, excitation, precond[None, :])


def pack_kernel(me_ref, wanted_ref, group_ref, out_ref):
    cols, places, exc, size = out_ref.shape
    rows = group_ref.shape[0]
    seg = group_ref.shape[1] // exc - 1
    slots = places - 1
    me = me_ref[0]
    tags = [group_ref[r, seg * exc :].astype(jnp.float32) for r in range(rows)]
    for p in range(cols):
        tag = jnp.concatenate([tag[p : p + 1] for tag in tags], axis=0)
        out_ref[p, slots] = tag.astype(jnp.bfloat16)

    def peer(p, _):
        line = ((me - p) & (cols - 1)) * 128
        for s in range(slots):
            block = wanted_ref[line + s] & (seg - 1)
            out_ref[p, s] = group_ref[s // TURNS, pl.ds(pl.multiple_of(block * exc, exc), exc), :]
        return 0

    lax.fori_loop(0, cols, peer, 0)


def pack(me, wanted, group, cols, exc):
    rows, _, size = group.shape
    return pl.pallas_call(
        pack_kernel,
        out_shape=jax.ShapeDtypeStruct((cols, rows * TURNS + 1, exc, size), jnp.bfloat16),
        in_specs=[SMEM, SMEM, VMEM],
        out_specs=VMEM,
        compiler_params=params(16),
        name="pack",
    )(me, wanted, group)


def near_kernel(count, me_ref, index_ref, blocks_ref, *rest):
    group_refs, outs, (weights_ref, sems, gather_ref) = rest[:count], rest[count:-3], rest[-3:]
    cols = len(outs)
    rows, per_row, _, size, _ = blocks_ref.shape
    seg, exc = outs[0].shape[:2]
    half = exc // 2
    me = me_ref[0]
    peers = [(me + k) & (cols - 1) for k in range(cols)]
    order = list(range(1, cols)) + [0]
    copies = {}
    for k in order:
        some = pl.ds(pl.multiple_of(peers[k] * seg, seg), seg)
        copies[k] = pltpu.make_async_copy(blocks_ref.at[some], weights_ref.at[k], sems.at[k])
        copies[k].start()
    group_ref = group_refs[0]
    if count > 1:
        group_ref = gather_ref
        x, y = lax.shift_right_arithmetic(me_ref[1], log2(count)), me_ref[1] & (count - 1)
        for i in range(count):
            for j in range(count):
                source = ((x - i) & (count - 1)) * count + ((y - j) & (count - 1))
                gather_ref[source] = group_refs[i][j]
    for k in order:
        copies[k].wait()
        for i in range(seg):
            parts = []
            for j in range(per_row):
                block = index_ref[j, peers[k] * seg + i]
                line = pl.multiple_of((block & (seg - 1)) * exc, exc)
                parts.append(
                    group_ref[lax.shift_right_arithmetic(block, log2(seg)), pl.ds(line, exc), :]
                )
            weights = [weights_ref[k, i, j].reshape(2 * size, size) for j in range(per_row)]
            total = dot_t(jnp.concatenate(parts, axis=1), jnp.concatenate(weights, axis=1))
            by_re, by_im = total[:, :size], total[:, size:]
            sums = [by_re[:half] - by_im[half:], by_re[half:] + by_im[:half]]
            outs[k][i] = jnp.concatenate(sums, axis=0).astype(outs[k].dtype)


def near_sums(me, index, blocks, groups, seg, exc):
    rows, per_row, _, size, _ = blocks.shape
    cols = rows // seg
    count = len(groups)
    gather = (count * count, seg * exc, size) if count > 1 else (1, exc, size)
    return pl.pallas_call(
        functools.partial(near_kernel, count),
        out_shape=[
            jax.ShapeDtypeStruct((seg, exc, size), jnp.bfloat16 if k else jnp.float32)
            for k in range(cols)
        ],
        in_specs=[SMEM, SMEM, pl.BlockSpec(memory_space=pl.ANY)] + [VMEM] * count,
        out_specs=[VMEM] * cols,
        scratch_shapes=[
            pltpu.VMEM((cols, seg) + blocks.shape[1:], jnp.bfloat16),
            pltpu.SemaphoreType.DMA((cols,)),
            pltpu.VMEM(gather, jnp.bfloat16),
        ],
        compiler_params=params(57),
        cost_estimate=pl.CostEstimate(
            flops=2 * exc * blocks.size, bytes_accessed=2 * blocks.size, transcendentals=0
        ),
        name="near",
    )(me, index, blocks, *groups)


def optics_kernel(
    forward_ref, back_ref, x_ref, reflect_ref, coupling_ref, facet_ref, out_ref, weights_ref, sems
):
    tiles, slots, _, facets, size = coupling_ref.shape
    exc = x_ref.shape[1]
    half = exc // 2
    group = 4
    free = back_ref[back_ref.shape[0] - 1]

    def fetch(t):
        return pltpu.make_async_copy(coupling_ref.at[t], weights_ref.at[t], sems.at[t])

    for t in range(tiles):
        fetch(t).start()

    def weights(t, v):
        pair = [weights_ref[t, u].reshape(2 * facets, size) for u in (v, v + 1)]
        return jnp.concatenate(pair, axis=1)

    def some(g, _):
        rounded = []
        for i in range(group):
            fetch(g * group + i).wait()
        for i in range(group):
            t = g * group + i
            total = None
            for v in range(0, slots, 2):
                parts = []
                for u in (v, v + 1):
                    slot = forward_ref[t * slots + u]
                    live = slot >= 0
                    x = x_ref[jnp.where(live, slot, 0)]
                    parts.append(jnp.where(live, x, jnp.zeros_like(x)))
                product = dot_t(jnp.concatenate(parts, axis=1), weights(t, v))
                total = product if total is None else total + product
            by_re, by_im = total[:, :facets], total[:, facets:]
            inc_re = by_re[:half] - by_im[half:]
            inc_im = by_re[half:] + by_im[:half]
            lanes = pl.ds(pl.multiple_of(t * facets, facets), facets)
            coef_re, coef_im = reflect_ref[0:1, lanes], reflect_ref[1:2, lanes]
            out_re = coef_re * inc_re - coef_im * inc_im
            out_im = coef_re * inc_im + coef_im * inc_re
            facet_ref[0, :, lanes] = out_re
            facet_ref[1, :, lanes] = out_im
            both = [
                jnp.concatenate([out_re, -out_im], axis=1),
                jnp.concatenate([out_im, out_re], axis=1),
            ]
            rounded.append(jnp.concatenate(both, axis=0).astype(jnp.bfloat16))
        for i in range(group):
            t = g * group + i
            for v in range(0, slots, 2):
                sums = jnp.dot(rounded[i], weights(t, v), preferred_element_type=jnp.float32)
                sums = sums.astype(jnp.bfloat16)
                for u in range(2):
                    slot = back_ref[t * slots + v + u]
                    slot = jnp.where(slot >= 0, slot, free)
                    out_ref[slot] = sums[:, u * size : (u + 1) * size]
        return 0

    lax.fori_loop(0, tiles // group, some, 0)


def optics(forward, back, coupling, x, reflect, devices):
    tiles, slots, _, facets, size = coupling.shape
    exc = x.shape[1]
    return pl.pallas_call(
        optics_kernel,
        out_shape=(
            jax.ShapeDtypeStruct((2, exc // 2, tiles * facets), jnp.float32),
            jax.ShapeDtypeStruct((devices * TURNS, exc, size), jnp.bfloat16),
        ),
        in_specs=[SMEM, SMEM, VMEM, VMEM, pl.BlockSpec(memory_space=pl.ANY)],
        out_specs=(VMEM, VMEM),
        scratch_shapes=[
            pltpu.VMEM(coupling.shape, jnp.bfloat16),
            pltpu.SemaphoreType.DMA((tiles,)),
        ],
        compiler_params=params(57),
        cost_estimate=pl.CostEstimate(
            flops=4 * exc * coupling.size, bytes_accessed=2 * coupling.size, transcendentals=0
        ),
        name="optics",
    )(forward, back, x, reflect, coupling)


def update_kernel(cols, tag_ref, back_ref, currents_ref, excitation_ref, precond_ref, *rest):
    near_refs, rest = rest[:cols], rest[cols:]
    out_ref, (total_ref, own_ref, sem) = rest[0], rest[-3:]
    own = pltpu.make_async_copy(near_refs[0], own_ref, sem)
    own.start()
    count, exc, size = back_ref.shape
    seg = near_refs[0].shape[0]
    half = exc // 2
    rows = count // (cols * TURNS)
    total = near_refs[1][...].astype(jnp.float32)
    for near_ref in near_refs[2:]:
        total += near_ref[...].astype(jnp.float32)
    total_ref[:seg] = total

    def seen(r):
        for c in range(cols):
            tag = tag_ref[c * rows + r]
            slot = (r * cols + c) * TURNS
            yield slot, lax.shift_right_arithmetic(tag, log2(2 * seg))
            yield slot + 1, tag & (2 * seg - 1)

    def add(r, _):
        for slot, block in seen(r):
            total_ref[block] = total_ref[block] + back_ref[slot].astype(jnp.float32)
        return 0

    lax.fori_loop(0, rows, add, 0)
    own.wait()
    for b in range(seg):
        lanes = slice(b * size, (b + 1) * size)
        scale = precond_ref[:, lanes]
        for q in range(2):
            some = slice(q * half, (q + 1) * half)
            part = total_ref[b, some] + own_ref[b, some]
            new = currents_ref[q, :, lanes] + scale * (excitation_ref[q, :, lanes] - part)
            out_ref[q, :, lanes] = new
            if len(rest) > 4:
                total_ref[b, some] = new
    if len(rest) > 4:
        rounded_ref, sent_ref = rest[1:3]
        for b in range(seg):
            rounded_ref[b * exc : (b + 1) * exc] = total_ref[b].astype(jnp.bfloat16)

        def fill(r, _):
            for slot, block in seen(r):
                line = pl.multiple_of((block & (seg - 1)) * exc, exc)
                sent_ref[slot] = rounded_ref[pl.ds(line, exc), :]
            return 0

        lax.fori_loop(0, rows, fill, 0)


def update(tags, back, near, currents, excitation, precond, last):
    seg, exc, size = near[0].shape
    out_shape = [jax.ShapeDtypeStruct(currents.shape, jnp.float32)]
    if not last:
        out_shape.append(jax.ShapeDtypeStruct((seg * exc, size), jnp.bfloat16))
        out_shape.append(jax.ShapeDtypeStruct(back.shape, jnp.bfloat16))
    return pl.pallas_call(
        functools.partial(update_kernel, len(near)),
        out_shape=out_shape,
        in_specs=[SMEM] + [VMEM] * 4 + [HBM] + [VMEM] * (len(near) - 1),
        out_specs=[VMEM] * len(out_shape),
        scratch_shapes=[
            pltpu.VMEM((seg + 1, exc, size), jnp.float32),
            pltpu.VMEM((seg, exc, size), jnp.float32),
            pltpu.SemaphoreType.DMA,
        ],
        compiler_params=params(16),
        name="update",
    )(tags, back, currents, excitation, precond[None, :], *near)


def along(x, k, cols):
    return lax.ppermute(x, "col", [(i, (i + k) % cols) for i in range(cols)])


def along_square(a, dx, dy, side):
    pairs = []
    for i in range(side):
        for j in range(side):
            pairs.append((i * side + j, (i + dx) % side * side + (j + dy) % side))
    return lax.ppermute(a, "row", pairs)


def all_devices(x, devices):
    slots, exc, size = x.shape
    sent = x.reshape(devices, slots // devices * exc, size)
    return lax.all_to_all(sent, ("row", "col"), 0, 0, tiled=True).reshape(x.shape)


def shards(excitation, precond, near_blocks, near_index, coupling, visible, reflect):
    exc = 2 * excitation.shape[1]
    size = coupling.shape[-1]
    seg = excitation.shape[2] // size
    rows, cols = lax.axis_size("row"), lax.axis_size("col")
    devices = rows * cols
    side = 1 << log2(rows) // 2

    me = jnp.stack([lax.axis_index("col"), lax.axis_index("row")]).astype(jnp.int32)
    forward, back, wanted, currents, copies = start(
        me, visible, excitation, precond, rows, cols, size
    )
    lines = [wanted[:1]]
    for k in range(1, cols):
        with jax.named_scope("wanted_exchange"):
            lines.append(along(wanted[k : k + 1], k, cols))
    wanted = jnp.concatenate(lines).reshape(-1)
    index = near_index[0].T
    rounded = sent = tags = None
    for iteration in range(ITERS):
        last = iteration == ITERS - 1
        if iteration == 0:
            with jax.named_scope("row_exchange"):
                groups = [lax.all_to_all(copies, "row", 0, 0, tiled=True)]
            packed = pack(me, wanted, groups[0], cols, exc)
            with jax.named_scope("col_exchange"):
                x = lax.all_to_all(packed, "col", 0, 0, tiled=True)
            tags = x[:, -1, :, 0].astype(jnp.int32).reshape(-1)
            x = x.reshape((-1,) + x.shape[2:])
        else:
            with jax.named_scope("forward_exchange"):
                x = all_devices(sent, devices)
            with jax.named_scope("row_gather"):
                line = [along_square(rounded, 0, k, side) for k in range(1, side)]
                x, line = lax.optimization_barrier((x, jnp.stack([rounded] + line)))
                groups = [line] + [along_square(line, k, 0, side) for k in range(1, side)]
            forward = back
        facets, sums = optics(forward, back, coupling, x, reflect, devices)
        sums, groups = lax.optimization_barrier((sums, groups))
        near = near_sums(me, index, near_blocks[0], groups, seg, exc)
        with jax.named_scope("near_exchange"):
            near = [near[0]] + [along(near[k], k, cols) for k in range(1, cols)]
        with jax.named_scope("back_exchange"):
            sums = all_devices(sums, devices)
        out = update(tags, sums, near, currents, excitation, precond, last)
        currents = out[0]
        if not last:
            rounded, sent = out[1:]
    return currents, facets


def solution(mesh):
    placed = (
        P(None, None, ("row", "col")),
        P(("row", "col")),
        P("col", "row", None, None, None, None),
        P("col", "row", None),
        P(("row", "col"), None, None, None, None),
        P(("row", "col"), None),
        P(None, ("row", "col")),
    )
    return jax.shard_map(
        shards,
        mesh=mesh,
        in_specs=placed,
        out_specs=(P(None, None, ("row", "col")), P(None, None, ("row", "col"))),
        check_vma=False,
    )
```

```python
import functools

import jax
import jax.numpy as jnp
from jax import lax
from jax.experimental import pallas as pl
from jax.experimental.pallas import tpu as pltpu
from jax.sharding import PartitionSpec as P

ITERS = 2
TURNS = 2
VMEM = pl.BlockSpec(memory_space=pltpu.VMEM)
SMEM = pl.BlockSpec(memory_space=pltpu.SMEM)
HBM = pl.BlockSpec(memory_space=pltpu.HBM)


def params(mib, **more):
    return pltpu.CompilerParams(vmem_limit_bytes=mib << 20, **more)


def dot_t(a, b):
    return lax.dot_general(a, b, (((1,), (1,)), ((), ())), preferred_element_type=jnp.float32)


def log2(n):
    return n.bit_length() - 1


def start_kernel(
    rows, cols, visible_in, excitation_in, precond_in,
    slot_out, wanted_ref, currents_ref, copies_out,
    count_ref, code_ref, visible_ref, excitation_ref, precond_ref, slot_ref, rounded_ref, tag_ref, sems,
):
    fetches = [
        pltpu.make_async_copy(visible_in, visible_ref, sems.at[0]),
        pltpu.make_async_copy(excitation_in, excitation_ref, sems.at[1]),
        pltpu.make_async_copy(precond_in, precond_ref, sems.at[2]),
    ]
    for fetch in fetches:
        fetch.start()
    slots, tiles = visible_ref.shape
    half, lanes = excitation_ref.shape[1:]
    exc, size = tag_ref.shape[1:]
    seg = lanes // size
    none = rows * cols
    base = 2 * seg

    def clear(i, _):
        count_ref[i] = 0
        code_ref[i] = seg * base + seg
        return 0

    lax.fori_loop(0, none + 1, clear, 0, unroll=8)
    for fetch in fetches[1:]:
        fetch.wait()
    for b in range(seg):
        at = slice(b * size, (b + 1) * size)
        parts = []
        for q in range(2):
            new = precond_ref[:, at] * excitation_ref[q, :, at]
            currents_ref[q, :, at] = new
            parts.append(new)
        rounded_ref[b * exc : (b + 1) * exc] = jnp.concatenate(parts, axis=0).astype(jnp.bfloat16)
    stores = [
        pltpu.make_async_copy(rounded_ref, copies_out.at[r, : seg * exc], sems.at[5 + r])
        for r in range(rows)
    ]
    for store in stores:
        store.start()
    fetches[0].wait()

    def tile(t, _):
        for v in range(slots):
            block = visible_ref[v, t]
            live = block >= 0
            owner = jnp.where(live, lax.shift_right_arithmetic(block, log2(seg)), none)
            turn = count_ref[owner]
            count_ref[owner] = turn + live.astype(jnp.int32)
            row = lax.shift_right_arithmetic(owner, log2(cols))
            col = owner & (cols - 1)
            slot_ref[t * slots + v] = jnp.where(live, owner * TURNS + turn, -1)
            mine = block & (seg - 1)
            wanted_ref[jnp.where(live, col, cols), row * TURNS + turn] = mine
            code_ref[owner] = code_ref[owner] + jnp.where(turn == 0, base, 1) * (mine - seg)
        return 0

    lax.fori_loop(0, tiles, tile, 0)
    line = lax.broadcasted_iota(jnp.int32, (exc, size), 0)

    def fill(r, _):
        tag = jnp.zeros((exc, size), jnp.float32)
        for c in range(cols):
            tag = jnp.where(line == c, code_ref[r * cols + c].astype(jnp.float32), tag)
        tag_ref[r] = tag.astype(jnp.bfloat16)
        return 0

    lax.fori_loop(0, rows, fill, 0)
    stores.append(pltpu.make_async_copy(tag_ref, copies_out.at[:, seg * exc :], sems.at[3]))
    stores[-1].start()

    def find(i, free):
        return jnp.where(count_ref[i] < TURNS, i * TURNS + TURNS - 1, free)

    slot_ref[tiles * slots] = lax.fori_loop(0, none, find, 0, unroll=8)
    stores.append(pltpu.make_async_copy(slot_ref, slot_out, sems.at[4]))
    stores[-1].start()
    for store in stores:
        store.wait()


def start(visible, excitation, precond, rows, cols, size):
    count = visible.size
    exc = 2 * excitation.shape[1]
    lines = excitation.shape[2] // size * exc
    return pl.pallas_call(
        functools.partial(start_kernel, rows, cols),
        out_shape=(
            jax.ShapeDtypeStruct((count + 1,), jnp.int32),
            jax.ShapeDtypeStruct((cols + 1, 128), jnp.int32),
            jax.ShapeDtypeStruct(excitation.shape, jnp.float32),
            jax.ShapeDtypeStruct((rows, lines + exc, size), jnp.bfloat16),
        ),
        in_specs=[HBM, HBM, HBM],
        out_specs=(HBM, SMEM, VMEM, HBM),
        compiler_params=params(64),
        scratch_shapes=[
            pltpu.SMEM((rows * cols + 1,), jnp.int32),
            pltpu.SMEM((rows * cols + 1,), jnp.int32),
            pltpu.SMEM(visible.shape[::-1], jnp.int32),
            pltpu.VMEM(excitation.shape, jnp.float32),
            pltpu.VMEM((1, precond.size), jnp.float32),
            pltpu.SMEM((count + 1,), jnp.int32),
            pltpu.VMEM((lines, size), jnp.bfloat16),
            pltpu.VMEM((rows, exc, size), jnp.bfloat16),
            pltpu.SemaphoreType.DMA((5 + rows,)),
        ],
        name="start",
    )(visible.T, excitation, precond[None, :])


def pack_kernel(me_ref, wanted_ref, group_ref, out_ref):
    cols, places, exc, size = out_ref.shape
    rows = group_ref.shape[0]
    seg = group_ref.shape[1] // exc - 1
    slots = places - 1
    me = me_ref[0]
    tags = [group_ref[r, seg * exc :].astype(jnp.float32) for r in range(rows)]
    for p in range(cols):
        tag = jnp.concatenate([tag[p : p + 1] for tag in tags], axis=0)
        out_ref[p, slots] = tag.astype(jnp.bfloat16)

    def peer(p, _):
        back = (lax.shift_right_arithmetic(me, 1) - lax.shift_right_arithmetic(p, 1)) & (cols // 2 - 1)
        line = ((back * 2 + ((p ^ me) & 1)) * cols + me) * 128
        for s in range(slots):
            block = wanted_ref[line + s] & (seg - 1)
            out_ref[p, s] = group_ref[s // TURNS, pl.ds(pl.multiple_of(block * exc, exc), exc), :]
        return 0

    lax.fori_loop(0, cols, peer, 0)


def pack(me, wanted, group, cols, exc):
    rows, _, size = group.shape
    return pl.pallas_call(
        pack_kernel,
        out_shape=jax.ShapeDtypeStruct((cols, rows * TURNS + 1, exc, size), jnp.bfloat16),
        in_specs=[SMEM, SMEM, VMEM],
        out_specs=VMEM,
        compiler_params=params(16),
        name="pack",
    )(me, wanted, group)


def near_kernel(count, me_ref, index_ref, blocks_ref, *rest):
    group_refs, outs, (weights_ref, sems, gather_ref) = rest[:count], rest[count:-3], rest[-3:]
    cols = len(outs)
    rows, per_row, _, size, _ = blocks_ref.shape
    seg, exc = outs[0].shape[:2]
    half = exc // 2
    me = me_ref[0]
    peers = [(me + k) & (cols - 1) for k in range(cols)]
    order = list(range(1, cols)) + [0]
    copies = {}
    for k in order:
        some = pl.ds(pl.multiple_of(peers[k] * seg, seg), seg)
        copies[k] = pltpu.make_async_copy(blocks_ref.at[some], weights_ref.at[k], sems.at[k])
        copies[k].start()
    group_ref = group_refs[0]
    if count > 1:
        group_ref = gather_ref
        x, y = lax.shift_right_arithmetic(me_ref[1], log2(count)), me_ref[1] & (count - 1)
        for i in range(count):
            for j in range(count):
                source = ((x - i) & (count - 1)) * count + ((y - j) & (count - 1))
                gather_ref[source] = group_refs[i][j]
    for k in order:
        copies[k].wait()
        for i in range(seg):
            parts = []
            for j in range(per_row):
                block = index_ref[j, peers[k] * seg + i]
                line = pl.multiple_of((block & (seg - 1)) * exc, exc)
                parts.append(
                    group_ref[lax.shift_right_arithmetic(block, log2(seg)), pl.ds(line, exc), :]
                )
            weights = [weights_ref[k, i, j].reshape(2 * size, size) for j in range(per_row)]
            total = dot_t(jnp.concatenate(parts, axis=1), jnp.concatenate(weights, axis=1))
            by_re, by_im = total[:, :size], total[:, size:]
            sums = [by_re[:half] - by_im[half:], by_re[half:] + by_im[:half]]
            outs[k][i] = jnp.concatenate(sums, axis=0).astype(outs[k].dtype)


def near_sums(me, index, blocks, groups, seg, exc):
    rows, per_row, _, size, _ = blocks.shape
    cols = rows // seg
    count = len(groups)
    gather = (count * count, seg * exc, size) if count > 1 else (1, exc, size)
    return pl.pallas_call(
        functools.partial(near_kernel, count),
        out_shape=[
            jax.ShapeDtypeStruct((seg, exc, size), jnp.bfloat16 if k else jnp.float32)
            for k in range(cols)
        ],
        in_specs=[SMEM, SMEM, pl.BlockSpec(memory_space=pl.ANY)] + [VMEM] * count,
        out_specs=[VMEM] * cols,
        scratch_shapes=[
            pltpu.VMEM((cols, seg) + blocks.shape[1:], jnp.bfloat16),
            pltpu.SemaphoreType.DMA((cols,)),
            pltpu.VMEM(gather, jnp.bfloat16),
        ],
        compiler_params=params(57),
        cost_estimate=pl.CostEstimate(
            flops=2 * exc * blocks.size, bytes_accessed=2 * blocks.size, transcendentals=0
        ),
        name="near",
    )(me, index, blocks, *groups)


def optics_kernel(
    rows, cols, by_column, slot_ref, reflect_ref, x_in, coupling_ref, facet_ref, out_ref,
    x_ref, weights_ref, sems,
):
    tiles, slots, _, facets, size = coupling_ref.shape
    exc = x_ref.shape[1]
    half = exc // 2
    group = 4
    free = slot_ref[tiles * slots]
    whole = pltpu.make_async_copy(x_in, x_ref, sems.at[tiles])
    whole.start()

    def place(slot):
        slot = jnp.maximum(slot, 0)
        if not by_column:
            return slot
        col = lax.shift_right_arithmetic(slot, log2(TURNS)) & (cols - 1)
        row = lax.shift_right_arithmetic(slot, log2(TURNS * cols))
        return col * (rows * TURNS + 1) + row * TURNS + (slot & (TURNS - 1))

    def fetch(t):
        return pltpu.make_async_copy(coupling_ref.at[t], weights_ref.at[t], sems.at[t])

    for t in range(tiles):
        fetch(t).start()
    whole.wait()

    def weights(t, v):
        pair = [weights_ref[t, u].reshape(2 * facets, size) for u in (v, v + 1)]
        return jnp.concatenate(pair, axis=1)

    def some(g, _):
        rounded = []
        for i in range(group):
            fetch(g * group + i).wait()
        for i in range(group):
            t = g * group + i
            total = None
            for v in range(0, slots, 2):
                parts = []
                for u in (v, v + 1):
                    slot = slot_ref[t * slots + u]
                    x = x_ref[place(slot)]
                    parts.append(jnp.where(slot >= 0, x, jnp.zeros_like(x)))
                product = dot_t(jnp.concatenate(parts, axis=1), weights(t, v))
                total = product if total is None else total + product
            by_re, by_im = total[:, :facets], total[:, facets:]
            inc_re = by_re[:half] - by_im[half:]
            inc_im = by_re[half:] + by_im[:half]
            lanes = pl.ds(pl.multiple_of(t * facets, facets), facets)
            coef_re, coef_im = reflect_ref[0:1, lanes], reflect_ref[1:2, lanes]
            out_re = coef_re * inc_re - coef_im * inc_im
            out_im = coef_re * inc_im + coef_im * inc_re
            facet_ref[0, :, lanes] = out_re
            facet_ref[1, :, lanes] = out_im
            both = [
                jnp.concatenate([out_re, -out_im], axis=1),
                jnp.concatenate([out_im, out_re], axis=1),
            ]
            rounded.append(jnp.concatenate(both, axis=0).astype(jnp.bfloat16))
        for i in range(group):
            t = g * group + i
            for v in range(0, slots, 2):
                sums = jnp.dot(rounded[i], weights(t, v), preferred_element_type=jnp.float32)
                sums = sums.astype(jnp.bfloat16)
                for u in range(2):
                    slot = slot_ref[t * slots + v + u]
                    slot = jnp.where(slot >= 0, slot, free)
                    out_ref[slot] = sums[:, u * size : (u + 1) * size]
        return 0

    lax.fori_loop(0, tiles // group, some, 0)


def optics(slots, coupling, x, reflect, rows, cols, by_column):
    tiles, _, _, facets, size = coupling.shape
    exc = x.shape[1]
    return pl.pallas_call(
        functools.partial(optics_kernel, rows, cols, by_column),
        out_shape=(
            jax.ShapeDtypeStruct((2, exc // 2, tiles * facets), jnp.float32),
            jax.ShapeDtypeStruct((rows * cols * TURNS, exc, size), jnp.bfloat16),
        ),
        in_specs=[SMEM, VMEM] + [pl.BlockSpec(memory_space=pl.ANY)] * 2,
        out_specs=(VMEM, VMEM),
        scratch_shapes=[
            pltpu.VMEM(x.shape, jnp.bfloat16),
            pltpu.VMEM(coupling.shape, jnp.bfloat16),
            pltpu.SemaphoreType.DMA((tiles + 1,)),
        ],
        compiler_params=params(57),
        cost_estimate=pl.CostEstimate(
            flops=4 * exc * coupling.size, bytes_accessed=2 * coupling.size, transcendentals=0
        ),
        name="optics",
    )(slots, reflect, x, coupling)


def update_kernel(cols, last, tag_ref, back_ref, currents_ref, excitation_ref, precond_ref, *rest):
    near_refs, rest = rest[:cols], rest[cols:]
    out_ref, (total_ref, *more_refs, own_ref, sem) = rest[0], rest[-6:]
    own = pltpu.make_async_copy(near_refs[0], own_ref, sem)
    own.start()
    count, exc, size = back_ref.shape
    seg = near_refs[0].shape[0]
    half = exc // 2
    rows = count // (cols * TURNS)
    total = near_refs[1][...].astype(jnp.float32)
    for near_ref in near_refs[2:]:
        total += near_ref[...].astype(jnp.float32)
    total_ref[:seg] = total
    for more_ref in more_refs:
        more_ref[...] = jnp.zeros_like(more_ref)

    def seen(r):
        for c in range(cols):
            tag = tag_ref[c * rows + r]
            slot = (r * cols + c) * TURNS
            yield slot, lax.shift_right_arithmetic(tag, log2(2 * seg))
            yield slot + 1, tag & (2 * seg - 1)

    def add(r, _):
        for i, (slot, block) in enumerate(seen(r)):
            sum_ref = (total_ref, *more_refs)[i % (1 + len(more_refs))]
            sum_ref[block] = sum_ref[block] + back_ref[slot].astype(jnp.float32)
        return 0

    lax.fori_loop(0, rows, add, 0)
    own.wait()
    for b in range(seg):
        lanes = slice(b * size, (b + 1) * size)
        scale = precond_ref[:, lanes]
        for q in range(2):
            some = slice(q * half, (q + 1) * half)
            part = total_ref[b, some] + own_ref[b, some]
            for more_ref in more_refs:
                part += more_ref[b, some]
            new = currents_ref[q, :, lanes] + scale * (excitation_ref[q, :, lanes] - part)
            out_ref[q, :, lanes] = new
            if not last:
                total_ref[b, some] = new
    if not last:
        rounded_ref, sent_ref = rest[1:3]
        for b in range(seg):
            rounded_ref[b * exc : (b + 1) * exc] = total_ref[b].astype(jnp.bfloat16)

        def fill(r, _):
            for slot, block in seen(r):
                line = pl.multiple_of((block & (seg - 1)) * exc, exc)
                sent_ref[slot] = rounded_ref[pl.ds(line, exc), :]
            return 0

        lax.fori_loop(0, rows, fill, 0)


def update(tags, back, near, currents, excitation, precond, last):
    seg, exc, size = near[0].shape
    out_shape = [jax.ShapeDtypeStruct(currents.shape, jnp.float32)]
    if not last:
        out_shape.append(jax.ShapeDtypeStruct((seg * exc, size), jnp.bfloat16))
        out_shape.append(jax.ShapeDtypeStruct(back.shape, jnp.bfloat16))
    return pl.pallas_call(
        functools.partial(update_kernel, len(near), last),
        out_shape=out_shape,
        in_specs=[SMEM] + [VMEM] * 4 + [HBM] + [VMEM] * (len(near) - 1),
        out_specs=[VMEM] * len(out_shape),
        scratch_shapes=[
            *[pltpu.VMEM((seg + 1, exc, size), jnp.float32)] * 4,
            pltpu.VMEM((seg, exc, size), jnp.float32),
            pltpu.SemaphoreType.DMA,
        ],
        compiler_params=params(16),
        name="update",
    )(tags, back, currents, excitation, precond[None, :], *near)


def along(x, k, cols):
    return lax.ppermute(x, "col", [(i, (i + k) % cols) for i in range(cols)])


def along_square(a, dx, dy, side):
    pairs = []
    for i in range(side):
        for j in range(side):
            pairs.append((i * side + j, (i + dx) % side * side + (j + dy) % side))
    return lax.ppermute(a, "row", pairs)


def all_devices(x, devices):
    slots, exc, size = x.shape
    sent = x.reshape(devices, slots // devices * exc, size)
    return lax.all_to_all(sent, ("row", "col"), 0, 0, tiled=True).reshape(x.shape)


def shards(excitation, precond, near_blocks, near_index, coupling, visible, reflect):
    exc = 2 * excitation.shape[1]
    size = coupling.shape[-1]
    seg = excitation.shape[2] // size
    rows, cols = lax.axis_size("row"), lax.axis_size("col")
    devices = rows * cols
    side = 1 << log2(rows) // 2

    me = jnp.stack([lax.axis_index("col"), lax.axis_index("row")]).astype(jnp.int32)
    slots, wanted, currents, copies = start(visible, excitation, precond, rows, cols, size)
    with jax.named_scope("wanted_exchange"):
        wanted = wanted[:cols]
        other = lax.ppermute(wanted, "col", [(i, i ^ 1) for i in range(cols)])
        pair = jnp.stack([wanted, other])
        wanted = jnp.stack([pair] + [along(pair, 2 * k, cols) for k in range(1, cols // 2)])
    wanted = wanted.reshape(-1)
    index = near_index[0].T
    rounded = sent = tags = None
    for iteration in range(ITERS):
        last = iteration == ITERS - 1
        if iteration == 0:
            with jax.named_scope("row_exchange"):
                groups = [lax.all_to_all(copies, "row", 0, 0, tiled=True)]
            packed = pack(me, wanted, groups[0], cols, exc)
            with jax.named_scope("col_exchange"):
                x = lax.all_to_all(packed, "col", 0, 0, tiled=True)
            tags = x[:, -1, :, 0].astype(jnp.int32).reshape(-1)
            x = x.reshape((-1,) + x.shape[2:])
        else:
            with jax.named_scope("forward_exchange"):
                x = all_devices(sent, devices)
            with jax.named_scope("row_gather"):
                line = [along_square(rounded, 0, k, side) for k in range(1, side)]
                x, line = lax.optimization_barrier((x, jnp.stack([rounded] + line)))
                groups = [line] + [along_square(line, k, 0, side) for k in range(1, side)]
        facets, sums = optics(slots, coupling, x, reflect, rows, cols, iteration == 0)
        sums, groups = lax.optimization_barrier((sums, groups))
        near = near_sums(me, index, near_blocks[0], groups, seg, exc)
        with jax.named_scope("near_exchange"):
            near = [near[0]] + [along(near[k], k, cols) for k in range(1, cols)]
        with jax.named_scope("back_exchange"):
            sums = all_devices(sums, devices)
        out = update(tags, sums, near, currents, excitation, precond, last)
        currents = out[0]
        if not last:
            rounded, sent = out[1:]
    return currents, facets


def solution(mesh):
    placed = (
        P(None, None, ("row", "col")),
        P(("row", "col")),
        P("col", "row", None, None, None, None),
        P("col", "row", None),
        P(("row", "col"), None, None, None, None),
        P(("row", "col"), None),
        P(None, ("row", "col")),
    )
    return jax.shard_map(
        shards,
        mesh=mesh,
        in_specs=placed,
        out_specs=(P(None, None, ("row", "col")), P(None, None, ("row", "col"))),
        check_vma=False,
    )
```

```python
import functools

import jax
import jax.numpy as jnp
from jax import lax
from jax.experimental import pallas as pl
from jax.experimental.pallas import tpu as pltpu
from jax.sharding import PartitionSpec as P

ITERS = 2
TURNS = 2
VMEM = pl.BlockSpec(memory_space=pltpu.VMEM)
SMEM = pl.BlockSpec(memory_space=pltpu.SMEM)
HBM = pl.BlockSpec(memory_space=pltpu.HBM)


def params(mib, **more):
    return pltpu.CompilerParams(vmem_limit_bytes=mib << 20, **more)


def dot_t(a, b):
    return lax.dot_general(a, b, (((1,), (1,)), ((), ())), preferred_element_type=jnp.float32)


def log2(n):
    return n.bit_length() - 1


def start_kernel(
    rows, cols, visible_in, excitation_in, precond_in,
    slot_out, wanted_out, currents_out, copies_out,
    code_ref, visible_ref, excitation_ref, precond_ref, slot_ref, wanted_ref, currents_ref,
    rounded_ref, tag_ref, sems,
):
    fetches = [
        pltpu.make_async_copy(visible_in, visible_ref, sems.at[0]),
        pltpu.make_async_copy(excitation_in, excitation_ref, sems.at[1]),
        pltpu.make_async_copy(precond_in, precond_ref, sems.at[2]),
    ]
    for fetch in fetches:
        fetch.start()
    slots, tiles = visible_ref.shape
    half, lanes = excitation_ref.shape[1:]
    exc, size = tag_ref.shape[1:]
    seg = lanes // size
    none = rows * cols
    base = 2 * seg

    def clear(i, _):
        code_ref[i] = seg * base + seg
        return 0

    lax.fori_loop(0, none + 1, clear, 0, unroll=8)
    for fetch in fetches[1:]:
        fetch.wait()
    for b in range(seg):
        at = slice(b * size, (b + 1) * size)
        parts = []
        for q in range(2):
            new = precond_ref[:, at] * excitation_ref[q, :, at]
            currents_ref[q, :, at] = new
            parts.append(new)
        rounded_ref[b * exc : (b + 1) * exc] = jnp.concatenate(parts, axis=0).astype(jnp.bfloat16)
    stores = [
        pltpu.make_async_copy(rounded_ref, copies_out.at[r, : seg * exc], sems.at[5 + r])
        for r in range(rows)
    ]
    stores.append(pltpu.make_async_copy(currents_ref, currents_out, sems.at[5 + rows]))
    for store in stores:
        store.start()
    fetches[0].wait()

    def tile(t, _):
        for v in range(slots):
            block = visible_ref[v, t]
            live = block >= 0
            owner = jnp.where(live, lax.shift_right_arithmetic(block, log2(seg)), none)
            code = code_ref[owner]
            turn = (code < seg * base).astype(jnp.int32)
            row = lax.shift_right_arithmetic(owner, log2(cols))
            col = owner & (cols - 1)
            slot_ref[t * slots + v] = jnp.where(live, owner * TURNS + turn, -1)
            mine = block & (seg - 1)
            wanted_ref[jnp.where(live, col, cols), row * TURNS + turn] = mine
            mine = mine - seg
            code_ref[owner] = code + jnp.where(turn == 0, mine * base, mine)
        return 0

    lax.fori_loop(0, tiles, tile, 0)
    line = lax.broadcasted_iota(jnp.int32, (exc, size), 0)

    def fill(r, _):
        tag = jnp.zeros((exc, size), jnp.float32)
        for c in range(cols):
            tag = jnp.where(line == c, code_ref[r * cols + c].astype(jnp.float32), tag)
        tag_ref[r] = tag.astype(jnp.bfloat16)
        return 0

    lax.fori_loop(0, rows, fill, 0)
    stores.append(pltpu.make_async_copy(tag_ref, copies_out.at[:, seg * exc :], sems.at[3]))
    stores[-1].start()
    stores.append(pltpu.make_async_copy(wanted_ref, wanted_out, sems.at[6 + rows]))
    stores[-1].start()

    def find(i, free):
        return jnp.where((code_ref[i] & (base - 1)) == seg, i * TURNS + TURNS - 1, free)

    slot_ref[tiles * slots] = lax.fori_loop(0, none, find, 0, unroll=8)
    stores.append(pltpu.make_async_copy(slot_ref, slot_out, sems.at[4]))
    stores[-1].start()
    for store in stores:
        store.wait()


def start(visible, excitation, precond, rows, cols, size):
    count = visible.size
    exc = 2 * excitation.shape[1]
    lines = excitation.shape[2] // size * exc
    return pl.pallas_call(
        functools.partial(start_kernel, rows, cols),
        out_shape=(
            jax.ShapeDtypeStruct((count + 1,), jnp.int32),
            jax.ShapeDtypeStruct((cols + 1, 128), jnp.int32),
            jax.ShapeDtypeStruct(excitation.shape, jnp.float32),
            jax.ShapeDtypeStruct((rows, lines + exc, size), jnp.bfloat16),
        ),
        in_specs=[HBM, HBM, HBM],
        out_specs=(HBM, HBM, HBM, HBM),
        compiler_params=params(64),
        scratch_shapes=[
            pltpu.SMEM((rows * cols + 1,), jnp.int32),
            pltpu.SMEM(visible.shape[::-1], jnp.int32),
            pltpu.VMEM(excitation.shape, jnp.float32),
            pltpu.VMEM((1, precond.size), jnp.float32),
            pltpu.SMEM((count + 1,), jnp.int32),
            pltpu.SMEM((cols + 1, 128), jnp.int32),
            pltpu.VMEM(excitation.shape, jnp.float32),
            pltpu.VMEM((lines, size), jnp.bfloat16),
            pltpu.VMEM((rows, exc, size), jnp.bfloat16),
            pltpu.SemaphoreType.DMA((7 + rows,)),
        ],
        name="start",
    )(visible.T, excitation, precond[None, :])


def pack_kernel(me_ref, wanted_ref, group_ref, out_ref):
    cols, places, exc, size = out_ref.shape
    rows = group_ref.shape[0]
    seg = group_ref.shape[1] // exc - 1
    slots = places - 1
    me = me_ref[0]
    tags = [group_ref[r, seg * exc :].astype(jnp.float32) for r in range(rows)]
    for p in range(cols):
        tag = jnp.concatenate([tag[p : p + 1] for tag in tags], axis=0)
        out_ref[p, slots] = tag.astype(jnp.bfloat16)

    def peer(p, _):
        back = (lax.shift_right_arithmetic(me, 1) - lax.shift_right_arithmetic(p, 1)) & (cols // 2 - 1)
        line = ((back * 2 + ((p ^ me) & 1)) * cols + me) * 128
        for s in range(slots):
            block = wanted_ref[line + s] & (seg - 1)
            out_ref[p, s] = group_ref[s // TURNS, pl.ds(pl.multiple_of(block * exc, exc), exc), :]
        return 0

    lax.fori_loop(0, cols, peer, 0)


def pack(me, wanted, group, cols, exc):
    rows, _, size = group.shape
    return pl.pallas_call(
        pack_kernel,
        out_shape=jax.ShapeDtypeStruct((cols, rows * TURNS + 1, exc, size), jnp.bfloat16),
        in_specs=[SMEM, SMEM, VMEM],
        out_specs=VMEM,
        compiler_params=params(16),
        name="pack",
    )(me, wanted, group)


def near_kernel(count, me_ref, index_ref, blocks_ref, *rest):
    group_refs, outs, (weights_ref, sems, gather_ref) = rest[:count], rest[count:-3], rest[-3:]
    cols = len(outs)
    rows, per_row, _, size, _ = blocks_ref.shape
    seg, exc = outs[0].shape[:2]
    half = exc // 2
    me = me_ref[0]
    peers = [(me + k) & (cols - 1) for k in range(cols)]
    order = list(range(1, cols)) + [0]
    copies = {}
    for k in order:
        some = pl.ds(pl.multiple_of(peers[k] * seg, seg), seg)
        copies[k] = pltpu.make_async_copy(blocks_ref.at[some], weights_ref.at[k], sems.at[k])
        copies[k].start()
    group_ref = group_refs[0]
    if count > 1:
        group_ref = gather_ref
        x, y = lax.shift_right_arithmetic(me_ref[1], log2(count)), me_ref[1] & (count - 1)
        for i in range(count):
            for j in range(count):
                source = ((x - i) & (count - 1)) * count + ((y - j) & (count - 1))
                gather_ref[source] = group_refs[i][j]
    for k in order:
        copies[k].wait()
        for i in range(seg):
            parts = []
            for j in range(per_row):
                block = index_ref[j, peers[k] * seg + i]
                line = pl.multiple_of((block & (seg - 1)) * exc, exc)
                parts.append(
                    group_ref[lax.shift_right_arithmetic(block, log2(seg)), pl.ds(line, exc), :]
                )
            weights = [weights_ref[k, i, j].reshape(2 * size, size) for j in range(per_row)]
            total = dot_t(jnp.concatenate(parts, axis=1), jnp.concatenate(weights, axis=1))
            by_re, by_im = total[:, :size], total[:, size:]
            sums = [by_re[:half] - by_im[half:], by_re[half:] + by_im[:half]]
            outs[k][i] = jnp.concatenate(sums, axis=0).astype(outs[k].dtype)


def near_sums(me, index, blocks, groups, seg, exc):
    rows, per_row, _, size, _ = blocks.shape
    cols = rows // seg
    count = len(groups)
    gather = (count * count, seg * exc, size) if count > 1 else (1, exc, size)
    return pl.pallas_call(
        functools.partial(near_kernel, count),
        out_shape=[
            jax.ShapeDtypeStruct((seg, exc, size), jnp.bfloat16 if k else jnp.float32)
            for k in range(cols)
        ],
        in_specs=[SMEM, SMEM, pl.BlockSpec(memory_space=pl.ANY)] + [VMEM] * count,
        out_specs=[VMEM] * cols,
        scratch_shapes=[
            pltpu.VMEM((cols, seg) + blocks.shape[1:], jnp.bfloat16),
            pltpu.SemaphoreType.DMA((cols,)),
            pltpu.VMEM(gather, jnp.bfloat16),
        ],
        compiler_params=params(57),
        cost_estimate=pl.CostEstimate(
            flops=2 * exc * blocks.size, bytes_accessed=2 * blocks.size, transcendentals=0
        ),
        name="near",
    )(me, index, blocks, *groups)


def optics_kernel(
    rows, cols, by_column, slot_in, reflect_in, x_in, coupling_ref, facet_out, out,
    slot_ref, reflect_ref, x_ref, weights_ref, facet_ref, out_ref, sems,
):
    tiles, slots, _, facets, size = coupling_ref.shape
    exc = x_ref.shape[1]
    half = exc // 2
    group = 4
    wholes = [
        pltpu.make_async_copy(slot_in, slot_ref, sems.at[tiles]),
        pltpu.make_async_copy(x_in, x_ref, sems.at[tiles + 1]),
        pltpu.make_async_copy(reflect_in, reflect_ref, sems.at[tiles + 2]),
    ]
    for whole in wholes:
        whole.start()

    def place(slot):
        slot = jnp.maximum(slot, 0)
        if not by_column:
            return slot
        col = lax.shift_right_arithmetic(slot, log2(TURNS)) & (cols - 1)
        row = lax.shift_right_arithmetic(slot, log2(TURNS * cols))
        return col * (rows * TURNS + 1) + row * TURNS + (slot & (TURNS - 1))

    def fetch(t):
        return pltpu.make_async_copy(coupling_ref.at[t], weights_ref.at[t], sems.at[t])

    for t in range(tiles):
        fetch(t).start()
    for whole in wholes:
        whole.wait()
    free = slot_ref[tiles * slots]

    def weights(t, v):
        pair = [weights_ref[t, u].reshape(2 * facets, size) for u in (v, v + 1)]
        return jnp.concatenate(pair, axis=1)

    def some(g, _):
        rounded = []
        for i in range(group):
            fetch(g * group + i).wait()
        for i in range(group):
            t = g * group + i
            total = None
            for v in range(0, slots, 2):
                parts = []
                for u in (v, v + 1):
                    slot = slot_ref[t * slots + u]
                    x = x_ref[place(slot)]
                    parts.append(jnp.where(slot >= 0, x, jnp.zeros_like(x)))
                product = dot_t(jnp.concatenate(parts, axis=1), weights(t, v))
                total = product if total is None else total + product
            by_re, by_im = total[:, :facets], total[:, facets:]
            inc_re = by_re[:half] - by_im[half:]
            inc_im = by_re[half:] + by_im[:half]
            lanes = pl.ds(pl.multiple_of(t * facets, facets), facets)
            coef_re, coef_im = reflect_ref[0:1, lanes], reflect_ref[1:2, lanes]
            out_re = coef_re * inc_re - coef_im * inc_im
            out_im = coef_re * inc_im + coef_im * inc_re
            facet_ref[0, :, lanes] = out_re
            facet_ref[1, :, lanes] = out_im
            both = [
                jnp.concatenate([out_re, -out_im], axis=1),
                jnp.concatenate([out_im, out_re], axis=1),
            ]
            rounded.append(jnp.concatenate(both, axis=0).astype(jnp.bfloat16))
        for i in range(group):
            t = g * group + i
            for v in range(0, slots, 2):
                sums = jnp.dot(rounded[i], weights(t, v), preferred_element_type=jnp.float32)
                sums = sums.astype(jnp.bfloat16)
                for u in range(2):
                    slot = slot_ref[t * slots + v + u]
                    slot = jnp.where(slot >= 0, slot, free)
                    out_ref[slot] = sums[:, u * size : (u + 1) * size]
        return 0

    lax.fori_loop(0, tiles // group, some, 0)
    stores = [
        pltpu.make_async_copy(out_ref, out, sems.at[0]),
        pltpu.make_async_copy(facet_ref, facet_out, sems.at[1]),
    ]
    for store in stores:
        store.start()
    for store in stores:
        store.wait()


def optics(slots, coupling, x, reflect, rows, cols, by_column):
    tiles, _, _, facets, size = coupling.shape
    exc = x.shape[1]
    facet_shape = (2, exc // 2, tiles * facets)
    out_shape = (rows * cols * TURNS, exc, size)
    return pl.pallas_call(
        functools.partial(optics_kernel, rows, cols, by_column),
        out_shape=(
            jax.ShapeDtypeStruct(facet_shape, jnp.float32),
            jax.ShapeDtypeStruct(out_shape, jnp.bfloat16),
        ),
        in_specs=[pl.BlockSpec(memory_space=pl.ANY)] * 4,
        out_specs=(HBM, HBM),
        scratch_shapes=[
            pltpu.SMEM(slots.shape, jnp.int32),
            pltpu.VMEM(reflect.shape, jnp.float32),
            pltpu.VMEM(x.shape, jnp.bfloat16),
            pltpu.VMEM(coupling.shape, jnp.bfloat16),
            pltpu.VMEM(facet_shape, jnp.float32),
            pltpu.VMEM(out_shape, jnp.bfloat16),
            pltpu.SemaphoreType.DMA((tiles + 3,)),
        ],
        compiler_params=params(57),
        cost_estimate=pl.CostEstimate(
            flops=4 * exc * coupling.size, bytes_accessed=2 * coupling.size, transcendentals=0
        ),
        name="optics",
    )(slots, reflect, x, coupling)


def update_kernel(cols, last, tag_ref, back_ref, currents_ref, excitation_ref, precond_ref, *rest):
    near_refs, rest = rest[:cols], rest[cols:]
    out_ref, (total_ref, *more_refs, own_ref, sem) = rest[0], rest[-6:]
    own = pltpu.make_async_copy(near_refs[0], own_ref, sem)
    own.start()
    count, exc, size = back_ref.shape
    seg = near_refs[0].shape[0]
    half = exc // 2
    rows = count // (cols * TURNS)
    total = near_refs[1][...].astype(jnp.float32)
    for near_ref in near_refs[2:]:
        total += near_ref[...].astype(jnp.float32)
    total_ref[:seg] = total
    for more_ref in more_refs:
        more_ref[...] = jnp.zeros_like(more_ref)

    def seen(r):
        for c in range(cols):
            tag = tag_ref[c * rows + r]
            slot = (r * cols + c) * TURNS
            yield slot, lax.shift_right_arithmetic(tag, log2(2 * seg))
            yield slot + 1, tag & (2 * seg - 1)

    def add(r, _):
        for i, (slot, block) in enumerate(seen(r)):
            sum_ref = (total_ref, *more_refs)[i % (1 + len(more_refs))]
            sum_ref[block] = sum_ref[block] + back_ref[slot].astype(jnp.float32)
        return 0

    lax.fori_loop(0, rows, add, 0)
    own.wait()
    for b in range(seg):
        lanes = slice(b * size, (b + 1) * size)
        scale = precond_ref[:, lanes]
        for q in range(2):
            some = slice(q * half, (q + 1) * half)
            part = total_ref[b, some] + own_ref[b, some]
            for more_ref in more_refs:
                part += more_ref[b, some]
            new = currents_ref[q, :, lanes] + scale * (excitation_ref[q, :, lanes] - part)
            out_ref[q, :, lanes] = new
            if not last:
                total_ref[b, some] = new
    if not last:
        rounded_ref, sent_ref = rest[1:3]
        for b in range(seg):
            rounded_ref[b * exc : (b + 1) * exc] = total_ref[b].astype(jnp.bfloat16)

        def fill(r, _):
            for slot, block in seen(r):
                line = pl.multiple_of((block & (seg - 1)) * exc, exc)
                sent_ref[slot] = rounded_ref[pl.ds(line, exc), :]
            return 0

        lax.fori_loop(0, rows, fill, 0)


def update(tags, back, near, currents, excitation, precond, last):
    seg, exc, size = near[0].shape
    out_shape = [jax.ShapeDtypeStruct(currents.shape, jnp.float32)]
    if not last:
        out_shape.append(jax.ShapeDtypeStruct((seg * exc, size), jnp.bfloat16))
        out_shape.append(jax.ShapeDtypeStruct(back.shape, jnp.bfloat16))
    return pl.pallas_call(
        functools.partial(update_kernel, len(near), last),
        out_shape=out_shape,
        in_specs=[SMEM] + [VMEM] * 4 + [HBM] + [VMEM] * (len(near) - 1),
        out_specs=[VMEM] * len(out_shape),
        scratch_shapes=[
            *[pltpu.VMEM((seg + 1, exc, size), jnp.float32)] * 4,
            pltpu.VMEM((seg, exc, size), jnp.float32),
            pltpu.SemaphoreType.DMA,
        ],
        compiler_params=params(16),
        name="update",
    )(tags, back, currents, excitation, precond[None, :], *near)


def along(x, k, cols):
    return lax.ppermute(x, "col", [(i, (i + k) % cols) for i in range(cols)])


def along_square(a, dx, dy, side):
    pairs = []
    for i in range(side):
        for j in range(side):
            pairs.append((i * side + j, (i + dx) % side * side + (j + dy) % side))
    return lax.ppermute(a, "row", pairs)


def all_devices(x, devices):
    slots, exc, size = x.shape
    sent = x.reshape(devices, slots // devices * exc, size)
    return lax.all_to_all(sent, ("row", "col"), 0, 0, tiled=True).reshape(x.shape)


def shards(excitation, precond, near_blocks, near_index, coupling, visible, reflect):
    exc = 2 * excitation.shape[1]
    size = coupling.shape[-1]
    seg = excitation.shape[2] // size
    rows, cols = lax.axis_size("row"), lax.axis_size("col")
    devices = rows * cols
    side = 1 << log2(rows) // 2

    me = jnp.stack([lax.axis_index("col"), lax.axis_index("row")]).astype(jnp.int32)
    slots, wanted, currents, copies = start(visible, excitation, precond, rows, cols, size)
    with jax.named_scope("wanted_exchange"):
        wanted = wanted[:cols]
        other = lax.ppermute(wanted, "col", [(i, i ^ 1) for i in range(cols)])
        pair = jnp.stack([wanted, other])
        wanted = jnp.stack([pair] + [along(pair, 2 * k, cols) for k in range(1, cols // 2)])
    wanted = wanted.reshape(-1)
    index = near_index[0].T
    rounded = sent = tags = None
    for iteration in range(ITERS):
        last = iteration == ITERS - 1
        if iteration == 0:
            with jax.named_scope("row_exchange"):
                groups = [lax.all_to_all(copies, "row", 0, 0, tiled=True)]
            packed = pack(me, wanted, groups[0], cols, exc)
            with jax.named_scope("col_exchange"):
                x = lax.all_to_all(packed, "col", 0, 0, tiled=True)
            tags = x[:, -1, :, 0].astype(jnp.int32).reshape(-1)
            x = x.reshape((-1,) + x.shape[2:])
        else:
            with jax.named_scope("forward_exchange"):
                x = all_devices(sent, devices)
            with jax.named_scope("row_gather"):
                line = [along_square(rounded, 0, k, side) for k in range(1, side)]
                x, line = lax.optimization_barrier((x, jnp.stack([rounded] + line)))
                groups = [line] + [along_square(line, k, 0, side) for k in range(1, side)]
        facets, sums = optics(slots, coupling, x, reflect, rows, cols, iteration == 0)
        sums, groups = lax.optimization_barrier((sums, groups))
        near = near_sums(me, index, near_blocks[0], groups, seg, exc)
        with jax.named_scope("near_exchange"):
            near = [near[0]] + [along(near[k], k, cols) for k in range(1, cols)]
        with jax.named_scope("back_exchange"):
            sums = all_devices(sums, devices)
        out = update(tags, sums, near, currents, excitation, precond, last)
        currents = out[0]
        if not last:
            rounded, sent = out[1:]
    return currents, facets


def solution(mesh):
    placed = (
        P(None, None, ("row", "col")),
        P(("row", "col")),
        P("col", "row", None, None, None, None),
        P("col", "row", None),
        P(("row", "col"), None, None, None, None),
        P(("row", "col"), None),
        P(None, ("row", "col")),
    )
    return jax.shard_map(
        shards,
        mesh=mesh,
        in_specs=placed,
        out_specs=(P(None, None, ("row", "col")), P(None, None, ("row", "col"))),
        check_vma=False,
    )
```

```python
import functools

import jax
import jax.numpy as jnp
from jax import lax
from jax.experimental import pallas as pl
from jax.experimental.pallas import tpu as pltpu
from jax.sharding import PartitionSpec as P

ITERS = 2
TURNS = 2
VMEM = pl.BlockSpec(memory_space=pltpu.VMEM)
SMEM = pl.BlockSpec(memory_space=pltpu.SMEM)
HBM = pl.BlockSpec(memory_space=pltpu.HBM)


def params(mib, **more):
    return pltpu.CompilerParams(vmem_limit_bytes=mib << 20, **more)


def dot_t(a, b):
    return lax.dot_general(a, b, (((1,), (1,)), ((), ())), preferred_element_type=jnp.float32)


def log2(n):
    return n.bit_length() - 1


def start_kernel(
    rows, cols, visible_in, excitation_in, precond_in,
    slot_out, wanted_out, currents_out, copies_out,
    code_ref, visible_ref, excitation_ref, precond_ref, slot_ref, wanted_ref, currents_ref,
    rounded_ref, tag_ref, sems,
):
    fetches = [
        pltpu.make_async_copy(visible_in, visible_ref, sems.at[0]),
        pltpu.make_async_copy(excitation_in, excitation_ref, sems.at[1]),
        pltpu.make_async_copy(precond_in, precond_ref, sems.at[2]),
    ]
    for fetch in fetches:
        fetch.start()
    slots, tiles = visible_ref.shape
    half, lanes = excitation_ref.shape[1:]
    exc, size = tag_ref.shape[1:]
    seg = lanes // size
    none = rows * cols
    base = 2 * seg

    def clear(i, _):
        code_ref[i] = seg * base + seg
        return 0

    lax.fori_loop(0, none + 1, clear, 0, unroll=8)
    for fetch in fetches[1:]:
        fetch.wait()
    for b in range(seg):
        at = slice(b * size, (b + 1) * size)
        parts = []
        for q in range(2):
            new = precond_ref[:, at] * excitation_ref[q, :, at]
            currents_ref[q, :, at] = new
            parts.append(new)
        rounded_ref[b * exc : (b + 1) * exc] = jnp.concatenate(parts, axis=0).astype(jnp.bfloat16)
    stores = [
        pltpu.make_async_copy(rounded_ref, copies_out.at[r, : seg * exc], sems.at[5 + r])
        for r in range(rows)
    ]
    stores.append(pltpu.make_async_copy(currents_ref, currents_out, sems.at[5 + rows]))
    for store in stores:
        store.start()
    fetches[0].wait()

    def tile(t, _):
        for v in range(slots):
            block = visible_ref[v, t]
            live = block >= 0
            owner = jnp.where(live, lax.shift_right_arithmetic(block, log2(seg)), none)
            code = code_ref[owner]
            turn = (code < seg * base).astype(jnp.int32)
            row = lax.shift_right_arithmetic(owner, log2(cols))
            col = owner & (cols - 1)
            slot_ref[t * slots + v] = jnp.where(live, owner * TURNS + turn, -1)
            mine = block & (seg - 1)
            wanted_ref[jnp.where(live, col, cols), row * TURNS + turn] = mine
            mine = mine - seg
            code_ref[owner] = code + jnp.where(turn == 0, mine * base, mine)
        return 0

    lax.fori_loop(0, tiles, tile, 0)
    line = lax.broadcasted_iota(jnp.int32, (exc, size), 0)

    def fill(r, _):
        tag = jnp.zeros((exc, size), jnp.float32)
        for c in range(cols):
            tag = jnp.where(line == c, code_ref[r * cols + c].astype(jnp.float32), tag)
        tag_ref[r] = tag.astype(jnp.bfloat16)
        return 0

    lax.fori_loop(0, rows, fill, 0)
    stores.append(pltpu.make_async_copy(tag_ref, copies_out.at[:, seg * exc :], sems.at[3]))
    stores[-1].start()
    stores.append(pltpu.make_async_copy(wanted_ref, wanted_out, sems.at[6 + rows]))
    stores[-1].start()

    def find(i, free):
        return jnp.where((code_ref[i] & (base - 1)) == seg, i * TURNS + TURNS - 1, free)

    slot_ref[tiles * slots] = lax.fori_loop(0, none, find, 0, unroll=8)
    stores.append(pltpu.make_async_copy(slot_ref, slot_out, sems.at[4]))
    stores[-1].start()
    for store in stores:
        store.wait()


def start(visible, excitation, precond, rows, cols, size):
    count = visible.size
    exc = 2 * excitation.shape[1]
    lines = excitation.shape[2] // size * exc
    return pl.pallas_call(
        functools.partial(start_kernel, rows, cols),
        out_shape=(
            jax.ShapeDtypeStruct((count + 1,), jnp.int32),
            jax.ShapeDtypeStruct((cols + 1, 128), jnp.int32),
            jax.ShapeDtypeStruct(excitation.shape, jnp.float32),
            jax.ShapeDtypeStruct((rows, lines + exc, size), jnp.bfloat16),
        ),
        in_specs=[HBM, HBM, HBM],
        out_specs=(HBM, HBM, HBM, HBM),
        compiler_params=params(64),
        scratch_shapes=[
            pltpu.SMEM((rows * cols + 1,), jnp.int32),
            pltpu.SMEM(visible.shape[::-1], jnp.int32),
            pltpu.VMEM(excitation.shape, jnp.float32),
            pltpu.VMEM((1, precond.size), jnp.float32),
            pltpu.SMEM((count + 1,), jnp.int32),
            pltpu.SMEM((cols + 1, 128), jnp.int32),
            pltpu.VMEM(excitation.shape, jnp.float32),
            pltpu.VMEM((lines, size), jnp.bfloat16),
            pltpu.VMEM((rows, exc, size), jnp.bfloat16),
            pltpu.SemaphoreType.DMA((7 + rows,)),
        ],
        name="start",
    )(visible.T, excitation, precond[None, :])


def pack_kernel(me_ref, wanted_ref, group_ref, out_ref):
    cols, places, exc, size = out_ref.shape
    rows = group_ref.shape[0]
    seg = group_ref.shape[1] // exc - 1
    slots = places - 1
    me = me_ref[0]
    tags = [group_ref[r, seg * exc :].astype(jnp.float32) for r in range(rows)]
    for p in range(cols):
        tag = jnp.concatenate([tag[p : p + 1] for tag in tags], axis=0)
        out_ref[p, slots] = tag.astype(jnp.bfloat16)

    def peer(p, _):
        back = (lax.shift_right_arithmetic(me, 1) - lax.shift_right_arithmetic(p, 1)) & (cols // 2 - 1)
        line = ((back * 2 + ((p ^ me) & 1)) * cols + me) * 128
        for s in range(slots):
            block = wanted_ref[line + s] & (seg - 1)
            out_ref[p, s] = group_ref[s // TURNS, pl.ds(pl.multiple_of(block * exc, exc), exc), :]
        return 0

    lax.fori_loop(0, cols, peer, 0)


def pack(me, wanted, group, cols, exc):
    rows, _, size = group.shape
    return pl.pallas_call(
        pack_kernel,
        out_shape=jax.ShapeDtypeStruct((cols, rows * TURNS + 1, exc, size), jnp.bfloat16),
        in_specs=[SMEM, SMEM, VMEM],
        out_specs=VMEM,
        compiler_params=params(16),
        name="pack",
    )(me, wanted, group)


def near_kernel(count, me_ref, index_ref, blocks_ref, *rest):
    groups, outs, (weights_ref, sems, group_ref) = rest[:count], rest[count:-3], rest[-3:]
    cols = len(outs)
    rows, per_row, _, size, _ = blocks_ref.shape
    seg, exc = outs[0].shape[:2]
    half = exc // 2
    me = me_ref[0]
    peers = [(me + k) & (cols - 1) for k in range(cols)]
    order = list(range(1, cols)) + [0]
    fetches = []
    if count == 1:
        fetches.append(pltpu.make_async_copy(groups[0], group_ref, sems.at[cols]))
    else:
        x, y = lax.shift_right_arithmetic(me_ref[1], log2(count)), me_ref[1] & (count - 1)
        for i in range(count):
            for j in range(count):
                source = ((x - i) & (count - 1)) * count + ((y - j) & (count - 1))
                sem = sems.at[cols + i * count + j]
                fetches.append(pltpu.make_async_copy(groups[i].at[j], group_ref.at[source], sem))
    for fetch in fetches:
        fetch.start()
    copies = {}
    for k in order:
        some = pl.ds(pl.multiple_of(peers[k] * seg, seg), seg)
        copies[k] = pltpu.make_async_copy(blocks_ref.at[some], weights_ref.at[k], sems.at[k])
        copies[k].start()
    for fetch in fetches:
        fetch.wait()
    for k in order:
        copies[k].wait()
        for i in range(seg):
            parts = []
            for j in range(per_row):
                block = index_ref[j, peers[k] * seg + i]
                line = pl.multiple_of((block & (seg - 1)) * exc, exc)
                parts.append(
                    group_ref[lax.shift_right_arithmetic(block, log2(seg)), pl.ds(line, exc), :]
                )
            weights = [weights_ref[k, i, j].reshape(2 * size, size) for j in range(per_row)]
            total = dot_t(jnp.concatenate(parts, axis=1), jnp.concatenate(weights, axis=1))
            by_re, by_im = total[:, :size], total[:, size:]
            sums = [by_re[:half] - by_im[half:], by_re[half:] + by_im[:half]]
            outs[k][i] = jnp.concatenate(sums, axis=0).astype(outs[k].dtype)


def near_sums(me, index, blocks, groups, seg, exc):
    rows, per_row, _, size, _ = blocks.shape
    cols = rows // seg
    count = len(groups)
    gather = (count * count, seg * exc, size) if count > 1 else groups[0].shape
    return pl.pallas_call(
        functools.partial(near_kernel, count),
        out_shape=[
            jax.ShapeDtypeStruct((seg, exc, size), jnp.bfloat16 if k else jnp.float32)
            for k in range(cols)
        ],
        in_specs=[SMEM, SMEM] + [pl.BlockSpec(memory_space=pl.ANY)] * (1 + count),
        out_specs=[VMEM] * cols,
        scratch_shapes=[
            pltpu.VMEM((cols, seg) + blocks.shape[1:], jnp.bfloat16),
            pltpu.SemaphoreType.DMA((cols + count * count,)),
            pltpu.VMEM(gather, jnp.bfloat16),
        ],
        compiler_params=params(57),
        cost_estimate=pl.CostEstimate(
            flops=2 * exc * blocks.size, bytes_accessed=2 * blocks.size, transcendentals=0
        ),
        name="near",
    )(me, index, blocks, *groups)


def optics_kernel(
    rows, cols, by_column, slot_in, reflect_in, x_in, coupling_ref, facet_out, out,
    slot_ref, reflect_ref, x_ref, weights_ref, facet_ref, out_ref, sems,
):
    tiles, slots, _, facets, size = coupling_ref.shape
    exc = x_ref.shape[1]
    half = exc // 2
    group = 4
    wholes = [
        pltpu.make_async_copy(slot_in, slot_ref, sems.at[tiles]),
        pltpu.make_async_copy(x_in, x_ref, sems.at[tiles + 1]),
        pltpu.make_async_copy(reflect_in, reflect_ref, sems.at[tiles + 2]),
    ]
    for whole in wholes:
        whole.start()

    def place(slot):
        slot = jnp.maximum(slot, 0)
        if not by_column:
            return slot
        col = lax.shift_right_arithmetic(slot, log2(TURNS)) & (cols - 1)
        row = lax.shift_right_arithmetic(slot, log2(TURNS * cols))
        return col * (rows * TURNS + 1) + row * TURNS + (slot & (TURNS - 1))

    def fetch(t):
        return pltpu.make_async_copy(coupling_ref.at[t], weights_ref.at[t], sems.at[t])

    for t in range(tiles):
        fetch(t).start()
    for whole in wholes:
        whole.wait()
    free = slot_ref[tiles * slots]

    def weights(t, v):
        pair = [weights_ref[t, u].reshape(2 * facets, size) for u in (v, v + 1)]
        return jnp.concatenate(pair, axis=1)

    def some(g, _):
        rounded = []
        for i in range(group):
            fetch(g * group + i).wait()
        for i in range(group):
            t = g * group + i
            total = None
            for v in range(0, slots, 2):
                parts = []
                for u in (v, v + 1):
                    slot = slot_ref[t * slots + u]
                    x = x_ref[place(slot)]
                    parts.append(jnp.where(slot >= 0, x, jnp.zeros_like(x)))
                product = dot_t(jnp.concatenate(parts, axis=1), weights(t, v))
                total = product if total is None else total + product
            by_re, by_im = total[:, :facets], total[:, facets:]
            inc_re = by_re[:half] - by_im[half:]
            inc_im = by_re[half:] + by_im[:half]
            lanes = pl.ds(pl.multiple_of(t * facets, facets), facets)
            coef_re, coef_im = reflect_ref[0:1, lanes], reflect_ref[1:2, lanes]
            out_re = coef_re * inc_re - coef_im * inc_im
            out_im = coef_re * inc_im + coef_im * inc_re
            facet_ref[0, :, lanes] = out_re
            facet_ref[1, :, lanes] = out_im
            both = [
                jnp.concatenate([out_re, -out_im], axis=1),
                jnp.concatenate([out_im, out_re], axis=1),
            ]
            rounded.append(jnp.concatenate(both, axis=0).astype(jnp.bfloat16))
        for i in range(group):
            t = g * group + i
            for v in range(0, slots, 2):
                sums = jnp.dot(rounded[i], weights(t, v), preferred_element_type=jnp.float32)
                sums = sums.astype(jnp.bfloat16)
                for u in range(2):
                    slot = slot_ref[t * slots + v + u]
                    slot = jnp.where(slot >= 0, slot, free)
                    out_ref[slot] = sums[:, u * size : (u + 1) * size]
        return 0

    lax.fori_loop(0, tiles // group, some, 0)
    stores = [
        pltpu.make_async_copy(out_ref, out, sems.at[0]),
        pltpu.make_async_copy(facet_ref, facet_out, sems.at[1]),
    ]
    for store in stores:
        store.start()
    for store in stores:
        store.wait()


def optics(slots, coupling, x, reflect, rows, cols, by_column):
    tiles, _, _, facets, size = coupling.shape
    exc = x.shape[1]
    facet_shape = (2, exc // 2, tiles * facets)
    out_shape = (rows * cols * TURNS, exc, size)
    return pl.pallas_call(
        functools.partial(optics_kernel, rows, cols, by_column),
        out_shape=(
            jax.ShapeDtypeStruct(facet_shape, jnp.float32),
            jax.ShapeDtypeStruct(out_shape, jnp.bfloat16),
        ),
        in_specs=[pl.BlockSpec(memory_space=pl.ANY)] * 4,
        out_specs=(HBM, HBM),
        scratch_shapes=[
            pltpu.SMEM(slots.shape, jnp.int32),
            pltpu.VMEM(reflect.shape, jnp.float32),
            pltpu.VMEM(x.shape, jnp.bfloat16),
            pltpu.VMEM(coupling.shape, jnp.bfloat16),
            pltpu.VMEM(facet_shape, jnp.float32),
            pltpu.VMEM(out_shape, jnp.bfloat16),
            pltpu.SemaphoreType.DMA((tiles + 3,)),
        ],
        compiler_params=params(57),
        cost_estimate=pl.CostEstimate(
            flops=4 * exc * coupling.size, bytes_accessed=2 * coupling.size, transcendentals=0
        ),
        name="optics",
    )(slots, reflect, x, coupling)


def update_kernel(cols, last, tag_ref, back_ref, currents_ref, excitation_ref, precond_ref, *rest):
    near_refs, rest = rest[:cols], rest[cols:]
    if not last:
        rest, more_last = rest[:-2], rest[-2:]
    out_ref, (total_ref, *more_refs, own_ref, sem) = rest[0], rest[-6:]
    own = pltpu.make_async_copy(near_refs[0], own_ref, sem)
    own.start()
    count, exc, size = back_ref.shape
    seg = near_refs[0].shape[0]
    half = exc // 2
    rows = count // (cols * TURNS)
    total = near_refs[1][...].astype(jnp.float32)
    for near_ref in near_refs[2:]:
        total += near_ref[...].astype(jnp.float32)
    total_ref[:seg] = total
    for more_ref in more_refs:
        more_ref[...] = jnp.zeros_like(more_ref)

    def seen(r):
        for c in range(cols):
            tag = tag_ref[c * rows + r]
            slot = (r * cols + c) * TURNS
            yield slot, lax.shift_right_arithmetic(tag, log2(2 * seg))
            yield slot + 1, tag & (2 * seg - 1)

    def add(r, _):
        for i, (slot, block) in enumerate(seen(r)):
            sum_ref = (total_ref, *more_refs)[i % (1 + len(more_refs))]
            sum_ref[block] = sum_ref[block] + back_ref[slot].astype(jnp.float32)
        return 0

    lax.fori_loop(0, rows, add, 0)
    own.wait()
    for b in range(seg):
        lanes = slice(b * size, (b + 1) * size)
        scale = precond_ref[:, lanes]
        for q in range(2):
            some = slice(q * half, (q + 1) * half)
            part = total_ref[b, some] + own_ref[b, some]
            for more_ref in more_refs:
                part += more_ref[b, some]
            new = currents_ref[q, :, lanes] + scale * (excitation_ref[q, :, lanes] - part)
            out_ref[q, :, lanes] = new
            if not last:
                total_ref[b, some] = new
    if not last:
        rounded_ref, sent_out = rest[1:3]
        sent_ref, sent_sems = more_last
        for b in range(seg):
            rounded_ref[b * exc : (b + 1) * exc] = total_ref[b].astype(jnp.bfloat16)

        def fill(r, _):
            for slot, block in seen(r):
                line = pl.multiple_of((block & (seg - 1)) * exc, exc)
                sent_ref[slot] = rounded_ref[pl.ds(line, exc), :]
            return 0

        stores = []
        for c in range(sent_sems.shape[0]):
            some_rows = rows // sent_sems.shape[0]
            lax.fori_loop(c * some_rows, (c + 1) * some_rows, fill, 0)
            part = pl.ds(c * some_rows * cols * TURNS, some_rows * cols * TURNS)
            stores.append(
                pltpu.make_async_copy(sent_ref.at[part], sent_out.at[part], sent_sems.at[c])
            )
            stores[-1].start()
        for store in stores:
            store.wait()


def update(tags, back, near, currents, excitation, precond, last):
    seg, exc, size = near[0].shape
    out_shape = [jax.ShapeDtypeStruct(currents.shape, jnp.float32)]
    if not last:
        out_shape.append(jax.ShapeDtypeStruct((seg * exc, size), jnp.bfloat16))
        out_shape.append(jax.ShapeDtypeStruct(back.shape, jnp.bfloat16))
    return pl.pallas_call(
        functools.partial(update_kernel, len(near), last),
        out_shape=out_shape,
        in_specs=[SMEM] + [VMEM] * 4 + [HBM] + [VMEM] * (len(near) - 1),
        out_specs=[VMEM] * len(out_shape) if last else [VMEM, VMEM, HBM],
        scratch_shapes=[
            *[pltpu.VMEM((seg + 1, exc, size), jnp.float32)] * 4,
            pltpu.VMEM((seg, exc, size), jnp.float32),
            pltpu.SemaphoreType.DMA,
        ]
        + ([] if last else [pltpu.VMEM(back.shape, jnp.bfloat16), pltpu.SemaphoreType.DMA((4,))]),
        compiler_params=params(16),
        name="update",
    )(tags, back, currents, excitation, precond[None, :], *near)


def along(x, k, cols):
    return lax.ppermute(x, "col", [(i, (i + k) % cols) for i in range(cols)])


def along_square(a, dx, dy, side):
    pairs = []
    for i in range(side):
        for j in range(side):
            pairs.append((i * side + j, (i + dx) % side * side + (j + dy) % side))
    return lax.ppermute(a, "row", pairs)


def all_devices(x, devices):
    slots, exc, size = x.shape
    sent = x.reshape(devices, slots // devices * exc, size)
    return lax.all_to_all(sent, ("row", "col"), 0, 0, tiled=True).reshape(x.shape)


def shards(excitation, precond, near_blocks, near_index, coupling, visible, reflect):
    exc = 2 * excitation.shape[1]
    size = coupling.shape[-1]
    seg = excitation.shape[2] // size
    rows, cols = lax.axis_size("row"), lax.axis_size("col")
    devices = rows * cols
    side = 1 << log2(rows) // 2

    me = jnp.stack([lax.axis_index("col"), lax.axis_index("row")]).astype(jnp.int32)
    slots, wanted, currents, copies = start(visible, excitation, precond, rows, cols, size)
    with jax.named_scope("wanted_exchange"):
        wanted = wanted[:cols]
        other = lax.ppermute(wanted, "col", [(i, i ^ 1) for i in range(cols)])
        pair = jnp.stack([wanted, other])
        wanted = jnp.stack([pair] + [along(pair, 2 * k, cols) for k in range(1, cols // 2)])
    wanted = wanted.reshape(-1)
    index = near_index[0].T
    rounded = sent = tags = None
    for iteration in range(ITERS):
        last = iteration == ITERS - 1
        if iteration == 0:
            with jax.named_scope("row_exchange"):
                groups = [lax.all_to_all(copies, "row", 0, 0, tiled=True)]
            packed = pack(me, wanted, groups[0], cols, exc)
            with jax.named_scope("col_exchange"):
                x = lax.all_to_all(packed, "col", 0, 0, tiled=True)
            tags = x[:, -1, :, 0].astype(jnp.int32).reshape(-1)
            x = x.reshape((-1,) + x.shape[2:])
        else:
            with jax.named_scope("forward_exchange"):
                x = all_devices(sent, devices)
            with jax.named_scope("row_gather"):
                line = [along_square(rounded, 0, k, side) for k in range(1, side)]
                x, line = lax.optimization_barrier((x, jnp.stack([rounded] + line)))
                groups = [line] + [along_square(line, k, 0, side) for k in range(1, side)]
        facets, sums = optics(slots, coupling, x, reflect, rows, cols, iteration == 0)
        sums, groups = lax.optimization_barrier((sums, groups))
        near = near_sums(me, index, near_blocks[0], groups, seg, exc)
        with jax.named_scope("near_exchange"):
            near = [near[0]] + [along(near[k], k, cols) for k in range(1, cols)]
        with jax.named_scope("back_exchange"):
            sums = all_devices(sums, devices)
        out = update(tags, sums, near, currents, excitation, precond, last)
        currents = out[0]
        if not last:
            rounded, sent = out[1:]
    return currents, facets


def solution(mesh):
    placed = (
        P(None, None, ("row", "col")),
        P(("row", "col")),
        P("col", "row", None, None, None, None),
        P("col", "row", None),
        P(("row", "col"), None, None, None, None),
        P(("row", "col"), None),
        P(None, ("row", "col")),
    )
    return jax.shard_map(
        shards,
        mesh=mesh,
        in_specs=placed,
        out_specs=(P(None, None, ("row", "col")), P(None, None, ("row", "col"))),
        check_vma=False,
    )
```
